128 devices in a mesh: tm: 8 (over x, core), dp: 8 (over y, z_lo), group: 2 (over z_hi).
Axes of the slice: x: 4, y: 4, z: 4 (z_hi: 2, z_lo: 2; z = z_hi * 2 + z_lo), core: 2. Of those that a mesh axis runs over, the one named last changes fastest.
Arguments:
- features: bfloat16 [16, 32, 256, 2048], P(('dp', 'group'), 'tm'), may hold values from -6 to 6
- conv_weight: bfloat16 [3, 256, 256], replicated, may hold values from -0.21875 to 0.21875
- out_weight: bfloat16 [48, 256], replicated, may hold values from -0.375 to 0.375
- first_weight: bfloat16 [3, 256, 48], replicated, may hold values from -0.5 to 0.5
- second_weight: bfloat16 [3, 256, 256], replicated, may hold values from -0.21875 to 0.21875
- head_weight: bfloat16 [256], replicated, may hold values from -0.375 to 0.375
- span_lengths: int32 [16, 4], P(('dp', 'group')), may hold values from 1 to 16, 32 in all within a row
- labels: int32 [16], P(('dp', 'group')), may hold values 0 or 1
Outputs:
- conv_grad: float32 [3, 256, 256], replicated
- out_grad: float32 [48, 256], replicated
- first_grad: float32 [3, 256, 48], replicated
- second_grad: float32 [3, 256, 256], replicated
- head_grad: float32 [256], replicated
The draws below stay inside these ranges and needn't reach their ends.
Inputs may be any that keep to these rules, and one draw needn't show every extreme that they name: `span_lengths`: each clip's 4 span lengths sum to 32; the longest is 16.
All inputs are finite; a program needn't handle non-finite values. No bound on the sum of `labels` on one device may be relied on, other than what follows from the above.
Results may differ from the reference program's by a relative error of at most 0.013.
The reference program's roundings to bfloat16 on the way (of `hidden`, `recon`, `disc_hidden`, `second_delta`, `first_delta`, `recon_grad` and `pre_delta`) count: a program that leaves them out, or rounds other values in their place, can miss the bound.
Values may be sent and summed in bfloat16 or wider, within the bound.
A program may use at most 192 MiB of HBM per device.

```python
import math
import jax
import jax.numpy as jnp
import numpy as np
from jax import lax

CHANNELS = 256
PATCH = 48
DISC = 256
SPANS = 4
POSITIONS = 2048
FRAMES = 32
CLIPS = 16


def with_ends(values, stream_key, smallest, top_value):
    dims = values.shape
    index_at = [jax.random.randint(jax.random.fold_in(stream_key, axis), (), 0, dims[axis]) for axis in range(len(dims))]
    values = values.at[tuple(index_at)].set(smallest)
    longest = dims.index(max(dims))
    index_at[longest] = (index_at[longest] + 1) % dims[longest]
    return values.at[tuple(index_at)].set(top_value)


def steps_of(key, shape, cuts, low, high):
    gain = 1.0
    for position, parts in cuts:
        draws = jax.random.uniform(jax.random.fold_in(jax.random.fold_in(key, 6), position), (parts,), jnp.float32, low / len(cuts), high / len(cuts))
        gain = gain * jnp.repeat(jnp.exp(draws), shape[position] // parts).reshape((-1,) + (1,) * (len(shape) - 1 - position))
    return gain


def profile(amount, total, reach, skew):
    loads = [(1 << 20) // math.isqrt(grade ** skew) + 1 for grade in range(2, amount + 1)]
    surplus, holding = total - reach - (amount - 1), [1] * (amount - 1)
    while surplus > 0:
        movable = [i for i in range(amount - 1) if holding[i] < reach]
        whole, budget = sum([loads[i] for i in movable]), surplus
        for i in movable:
            addition = min(reach - holding[i], max(1, budget * loads[i] // whole), surplus)
            holding[i] = holding[i] + addition
            surplus = surplus - addition
    return np.array([reach] + holding)


def ragged_sizes(own_key, number_of, total, most, lean):
    if number_of == 2:
        one = jax.random.randint(own_key, (), max(1, total - most), min(most, total - 1) + 1)
        return jnp.stack([one, total - one])
    tallies = jnp.asarray(profile(number_of, total, most, lean), jnp.int32)
    twos = (number_of - 1) // 2
    source_of, taker = tallies[1:1 + 2 * twos:2], tallies[2:2 + 2 * twos:2]
    room = jnp.minimum(source_of - 1, most - taker)
    shifted = jax.random.randint(jax.random.fold_in(own_key, 1), (twos,), 0, 1 << 20) % (room + 1)
    tallies = tallies.at[1:1 + 2 * twos:2].set(source_of - shifted).at[2:2 + 2 * twos:2].set(taker + shifted)
    return tallies[jax.random.permutation(jax.random.fold_in(own_key, 2), number_of)]


def gaussian(rng, shape, scale, bound, shards=(), held_as=jnp.bfloat16):
    loudness = steps_of(rng, shape, shards, -0.22, 0.18) if shards else 1.0
    values = jax.random.normal(rng, shape, jnp.float32) * scale * loudness
    return jnp.minimum(jnp.maximum(values, -bound), bound).astype(held_as)


def setup_inputs(seed: int = 0) -> dict:
    splits = jax.random.split(jax.random.key(seed), 9)
    return {
        "features": gaussian(splits[0], (CLIPS, FRAMES, CHANNELS, POSITIONS), 1.0, 6.0, ((0, 16), (1, 8))),
        "conv_weight": gaussian(splits[1], (3, CHANNELS, CHANNELS), (3 * CHANNELS) ** -0.5, 0.21875),
        "out_weight": gaussian(splits[2], (PATCH, CHANNELS), CHANNELS ** -0.5, 0.375),
        "first_weight": gaussian(splits[3], (3, DISC, PATCH), (3 * PATCH) ** -0.5, 0.5),
        "second_weight": gaussian(splits[4], (3, DISC, DISC), (3 * DISC) ** -0.5, 0.21875),
        "head_weight": gaussian(splits[5], (DISC,), DISC ** -0.5, 0.375),
        "span_lengths": jax.vmap(lambda own: ragged_sizes(own, SPANS, FRAMES, FRAMES // 2, 1))(jax.random.split(splits[6], CLIPS)).reshape((CLIPS, SPANS)).astype(jnp.int32),
        "labels": with_ends((jax.random.randint(splits[7], (CLIPS,), 0, 2) < 1).astype(jnp.int32), jax.random.fold_in(splits[7], 1), 0, 1),
    }


def leaky_relu(values):
    return jnp.where(values > 0, values, 0.2 * values)


def leaky_slope(values):
    return jnp.where(values > 0, 1.0, 0.2).astype(jnp.float32)


def round_half(values):
    return lax.optimization_barrier(values.astype(jnp.bfloat16)).astype(jnp.float32)


def span_masks(span_lengths, first_frame, frame_count):
    span_ends = jnp.cumsum(span_lengths, axis=1)
    positions = first_frame + jnp.arange(-2, frame_count, dtype=jnp.int32)
    segment = jnp.sum((positions[None, :, None] >= span_ends[:, None, :]).astype(jnp.int32), axis=2)
    current = segment[:, 2:]
    result = []
    for offset in range(3):
        earlier = segment[:, 2 - offset:2 - offset + frame_count]
        inside = positions[2 - offset:2 - offset + frame_count] >= 0
        result.append(((earlier == current) & inside[None, :]).astype(jnp.float32))
    return result


def one_clip(conv_weight, out_weight, first_weight, second_weight, head_weight, loss_scale, inputs):
    feature, lengths_row, label = inputs
    feature = feature[None].astype(jnp.float32)
    frame_count = feature.shape[1]
    tap_masks = span_masks(lengths_row[None], 0, frame_count)
    extended = jnp.pad(feature, ((0, 0), (2, 0), (0, 0), (0, 0)))
    conv_float = conv_weight.astype(jnp.float32)
    pre = sum(tap_masks[offset][:, :, None, None] * jnp.einsum("oi,btis->btos", conv_float[offset], extended[:, 2 - offset:2 - offset + frame_count]) for offset in range(3))
    hidden = round_half(feature + jax.nn.silu(pre))
    out_float = out_weight.astype(jnp.float32)
    recon = round_half(jnp.einsum("pc,btcs->btps", out_float, hidden))
    first_float = first_weight.astype(jnp.float32)
    second_float = second_weight.astype(jnp.float32)
    head_float = head_weight.astype(jnp.float32)
    padded = jnp.pad(recon, ((0, 0), (1, 1), (0, 0), (0, 0)))
    first_pre = sum(jnp.einsum("ep,btps->btes", first_float[offset], padded[:, offset:offset + frame_count]) for offset in range(3))
    disc_hidden = round_half(leaky_relu(first_pre))
    hidden_padded = jnp.pad(disc_hidden, ((0, 0), (1, 1), (0, 0), (0, 0)))
    second_pre = sum(jnp.einsum("fe,btes->btfs", second_float[offset], hidden_padded[:, offset:offset + frame_count]) for offset in range(3))
    second_act = leaky_relu(second_pre)
    logits = jnp.einsum("f,btfs->bts", head_float, second_act)
    signed = (2 * label - 1).astype(jnp.float32)
    logit_grad = -signed * jax.nn.sigmoid(-signed * logits) * loss_scale
    head_grad = jnp.einsum("bts,btfs->f", logit_grad, second_act)
    second_delta = round_half(logit_grad[:, :, None, :] * head_float[None, None, :, None] * leaky_slope(second_pre))
    second_grad = jnp.stack([jnp.einsum("btfs,btes->fe", second_delta, hidden_padded[:, offset:offset + frame_count]) for offset in range(3)])
    delta_padded = jnp.pad(second_delta, ((0, 0), (1, 1), (0, 0), (0, 0)))
    hidden_grad = sum(jnp.einsum("fe,btfs->btes", second_float[offset], delta_padded[:, 2 - offset:2 - offset + frame_count]) for offset in range(3))
    first_delta = round_half(hidden_grad * leaky_slope(first_pre))
    first_grad = jnp.stack([jnp.einsum("btes,btps->ep", first_delta, padded[:, offset:offset + frame_count]) for offset in range(3)])
    first_padded = jnp.pad(first_delta, ((0, 0), (1, 1), (0, 0), (0, 0)))
    recon_grad = round_half(sum(jnp.einsum("ep,btes->btps", first_float[offset], first_padded[:, 2 - offset:2 - offset + frame_count]) for offset in range(3)))
    out_grad = jnp.einsum("btps,btcs->pc", recon_grad, hidden)
    hidden_delta = jnp.einsum("pc,btps->btcs", out_float, recon_grad)
    gating = jax.nn.sigmoid(pre)
    pre_delta = round_half(hidden_delta * gating * (1.0 + pre * (1.0 - gating)))
    conv_grad = jnp.stack([jnp.einsum("btos,btis->oi", pre_delta * tap_masks[offset][:, :, None, None], extended[:, 2 - offset:2 - offset + frame_count]) for offset in range(3)])
    return conv_grad, out_grad, first_grad, second_grad, head_grad


def reference(features, conv_weight, out_weight, first_weight, second_weight, head_weight, span_lengths, labels):
    loss_scale = float(CLIPS * FRAMES * POSITIONS) ** -0.5

    def per_clip(inputs):
        return one_clip(conv_weight, out_weight, first_weight, second_weight, head_weight, loss_scale, inputs)

    stacked = lax.map(per_clip, (features, span_lengths, labels))
    conv_grad, out_grad, first_grad, second_grad, head_grad = [jnp.sum(member, axis=0) for member in stacked]
    return (conv_grad, out_grad, first_grad, second_grad, head_grad)
```

```python
import functools

import jax
import jax.numpy as jnp
from jax import lax
from jax.experimental import pallas as pl
from jax.experimental.pallas import tpu as pltpu
from jax.sharding import PartitionSpec as P

MESH = pl.DeviceIdType.MESH
F32 = jnp.float32


class Place:
    def __init__(self):
        tm, dp, group = (lax.axis_index(name) for name in ("tm", "dp", "group"))
        self.core = lax.rem(tm, 2)
        self.at = (tm // 2, dp // 2, 2 * group + lax.rem(dp, 2))

    def device(self, x, y, z, core):
        return (2 * x + core, 2 * y + lax.rem(z, 2), z // 2)

    def along(self, axis, step):
        place = list(self.at)
        place[axis] = lax.rem(place[axis] + step, 4)
        return self.device(*place, self.core)

    def other_core(self):
        return self.device(*self.at, 1 - self.core)


class Reducer:
    def __init__(self, place, grads, halves, total, bufs, send_sems, recv_sems):
        self.place, self.grads, self.halves, self.total = (place, grads, halves, total)
        self.core_in, self.sum1, self.in1, self.sum2, self.in2, self.in3 = bufs
        self.send_sems, self.recv_sems = (send_sems, recv_sems)
        self.rows = grads.shape[1]
        self.sent = []
        self.axes = [tuple((part + i) % 3 for i in range(3)) for part in range(3)]

    def copy(self, src, dst, slot, device):
        return pltpu.make_async_remote_copy(
            src_ref=src,
            dst_ref=dst,
            send_sem=self.send_sems.at[slot],
            recv_sem=self.recv_sems.at[slot],
            device_id=device,
            device_id_type=MESH,
        )

    def start(self, *args):
        copy = self.copy(*args)
        copy.start()
        self.sent.append(copy)

    def lanes(self, core):
        return pl.ds(pl.multiple_of(core * 128, 128), 128)

    def block(self, index, size):
        return pl.ds(pl.multiple_of(index * size, size), size)

    def slot(self, stage, part, step):
        return 3 + (stage * 3 + part) * 3 + step - 1

    def core_send(self, part):
        place = self.place
        src = self.grads.at[part, :, self.lanes(1 - place.core)]
        self.start(src, self.core_in.at[part], part, place.other_core())

    def core_sum(self, part):
        place = self.place
        self.copy(self.core_in.at[part], self.core_in.at[part], part, place.other_core()).wait_recv()
        self.sum1[part] = self.grads[part, :, self.lanes(place.core)] + self.core_in[part]

    def scatter_send(self, part, level):
        axis = self.axes[part][level]
        source, landing = ((self.sum1, self.in1), (self.sum2, self.in2))[level]
        size = landing.shape[2]
        for step in (1, 2, 3):
            target = lax.rem(self.place.at[axis] + step, 4)
            self.start(
                source.at[part, self.block(target, size)],
                landing.at[part, step - 1],
                self.slot(level, part, step),
                self.place.along(axis, step),
            )

    def scatter_sum(self, part, level):
        axis = self.axes[part][level]
        source, landing = ((self.sum1, self.in1), (self.sum2, self.in2))[level]
        size = landing.shape[2]
        for step in (1, 2, 3):
            here = landing.at[part, step - 1]
            self.copy(here, here, self.slot(level, part, step), self.place.along(axis, step)).wait_recv()
        result = source[part, self.block(self.place.at[axis], size)]
        for step in (1, 2, 3):
            result = result + landing[part, step - 1]
        if level == 0:
            self.sum2[part] = result
        else:
            self.in3[part, self.place.at[self.axes[part][2]]] = result

    def swap_send(self, part):
        axis = self.axes[part][2]
        here = self.in3.at[part, self.place.at[axis]]
        for step in (1, 2, 3):
            self.start(here, here, self.slot(2, part, step), self.place.along(axis, step))

    def rows_of(self, part, level):
        first = self.place.at[self.axes[part][0]]
        if level == 0:
            return self.block(first, self.rows // 4)
        return self.block(4 * first + self.place.at[self.axes[part][1]], self.rows // 16)

    def swap_sum(self, part):
        axis = self.axes[part][2]
        for step in (1, 2, 3):
            here = self.in3.at[part, step]
            self.copy(here, here, self.slot(2, part, step), self.place.along(axis, step)).wait_recv()
        result = (self.in3[part, 0] + self.in3[part, 1]) + (self.in3[part, 2] + self.in3[part, 3])
        self.total[part, self.rows_of(part, 1), self.lanes(self.place.core)] = result.astype(self.total.dtype)

    def gather_send(self, part, level):
        axis = self.axes[part][level]
        here = self.total.at[part, self.rows_of(part, level), self.lanes(self.place.core)]
        for step in (1, 2, 3):
            self.start(here, here, self.slot(4 - level, part, step), self.place.along(axis, step))

    def gather_wait(self, part, level):
        axis = self.axes[part][level]
        here = self.total.at[part, self.rows_of(part, level), self.lanes(self.place.core)]
        for step in (1, 2, 3):
            self.copy(here, here, self.slot(4 - level, part, step), self.place.along(axis, step)).wait_recv()

    def back_send(self, part):
        here = self.total.at[part, :, self.lanes(self.place.core)]
        self.start(here, here, 48 + part, self.place.other_core())

    def back_wait(self, part):
        here = self.total.at[part, :, self.lanes(1 - self.place.core)]
        self.copy(here, here, 48 + part, self.place.other_core()).wait_recv()

    def steps(self):
        def each(*calls):
            def run():
                for part in range(3):
                    for call, *level in calls:
                        call(part, *level)

            return run

        return [
            each((self.core_send,)),
            each((self.core_sum,), (self.scatter_send, 0)),
            each((self.scatter_sum, 0), (self.scatter_send, 1)),
            each((self.scatter_sum, 1), (self.swap_send,)),
            each((self.swap_sum,), (self.gather_send, 1)),
            each((self.gather_wait, 1), (self.gather_send, 0)),
            each((self.gather_wait, 0), (self.back_send,)),
            each((self.back_wait,)),
        ]

    def finish(self):
        for copy in self.sent:
            copy.wait_send()


N_SLOTS = 51


def reduce_scratch(rows):
    return [
        pltpu.VMEM((3, rows, 128), F32),
        pltpu.VMEM((3, rows, 128), F32),
        pltpu.VMEM((3, 3, rows // 4, 128), F32),
        pltpu.VMEM((3, rows // 4, 128), F32),
        pltpu.VMEM((3, 3, rows // 16, 128), F32),
        pltpu.VMEM((3, 4, rows // 16, 128), F32),
    ]


def greet(place):
    barrier = pltpu.get_barrier_semaphore()
    others = [place.other_core()] + [place.along(axis, step) for axis in range(3) for step in (1, 2, 3)]
    for device in others:
        pl.semaphore_signal(barrier, inc=1, device_id=device, device_id_type=MESH)
    pl.semaphore_wait(barrier, len(others))


def reduce_kernel(grads, total, *scratch):
    bufs, (send_sems, recv_sems) = scratch[:6], scratch[6:]
    place = Place()
    greet(place)
    reducer = Reducer(place, grads, None, total, bufs, send_sems, recv_sems)
    for step in reducer.steps():
        step()
    reducer.finish()


def all_sum(grads):
    rows = grads.shape[1]
    return pl.pallas_call(
        reduce_kernel,
        out_shape=jax.ShapeDtypeStruct(grads.shape, F32),
        in_specs=[pl.BlockSpec(memory_space=pltpu.VMEM)],
        out_specs=pl.BlockSpec(memory_space=pltpu.VMEM),
        scratch_shapes=reduce_scratch(rows)
        + [pltpu.SemaphoreType.DMA((N_SLOTS,)), pltpu.SemaphoreType.DMA((N_SLOTS,))],
        compiler_params=pltpu.CompilerParams(
            collective_id=0, has_side_effects=True, vmem_limit_bytes=32 * 1024 * 1024
        ),
    )(grads)


def shifted(value, axis, steps):
    count = lax.axis_size(axis)
    first, last = (max(0, -steps), min(count, count - steps))
    return lax.ppermute(value, axis, [(source, source + steps) for source in range(first, last)])


def with_halo(block, sides, width):
    for axis, dim in sides:
        count = lax.axis_size(axis)
        forward = [(i, i + 1) for i in range(count - 1)]
        backward = [(target, source) for source, target in forward]
        low = lax.ppermute(
            lax.slice_in_dim(block, block.shape[dim] - width, None, axis=dim), axis, forward
        )
        high = lax.ppermute(lax.slice_in_dim(block, 0, width, axis=dim), axis, backward)
        block = jnp.concatenate([low, block, high], axis=dim)
    return block


def leaky_relu(values):
    return jnp.where(values > 0, values, 0.2 * values)


def leaky_slope(values):
    return jnp.where(values > 0, 1.0, 0.2).astype(jnp.float32)


def span_masks(span_lengths, first_frame, frame_count):
    span_ends = jnp.cumsum(span_lengths, axis=1)
    positions = first_frame + jnp.arange(-2, frame_count, dtype=jnp.int32)
    segment = jnp.sum((positions[None, :, None] >= span_ends[:, None, :]).astype(jnp.int32), axis=2)
    current = segment[:, 2:]
    result = []
    for offset in range(3):
        earlier = segment[:, 2 - offset : 2 - offset + frame_count]
        inside = positions[2 - offset : 2 - offset + frame_count] >= 0
        result.append(((earlier == current) & inside[None, :]).astype(jnp.float32))
    return result


def discriminate(
    recon,
    first_weight,
    second_weight,
    head_weight,
    labels,
    loss_scale,
    pad_input,
    pad_hidden,
    pad_second,
    pad_first,
):
    frame_count = recon.shape[1]
    padded = pad_input(recon)
    first_pre = sum(
        (
            jnp.einsum(
                "ep,btps->btes",
                first_weight[offset],
                padded[:, offset : offset + frame_count],
                preferred_element_type=jnp.float32,
            )
            for offset in range(3)
        )
    )
    disc_hidden = leaky_relu(first_pre).astype(jnp.bfloat16)
    hidden_padded = pad_hidden(disc_hidden)
    second_pre = sum(
        (
            jnp.einsum(
                "fe,btes->btfs",
                second_weight[offset],
                hidden_padded[:, offset : offset + frame_count],
                preferred_element_type=jnp.float32,
            )
            for offset in range(3)
        )
    )
    second_act = leaky_relu(second_pre)
    head_float = head_weight.astype(jnp.float32)
    logits = jnp.einsum("f,btfs->bts", head_float, second_act)
    signed = (2 * labels - 1).astype(jnp.float32)[:, None, None]
    logit_grad = -signed * jax.nn.sigmoid(-signed * logits) * loss_scale
    head_grad = jnp.einsum("bts,btfs->f", logit_grad, second_act)
    second_delta = (
        logit_grad[:, :, None, :] * head_float[None, None, :, None] * leaky_slope(second_pre)
    ).astype(jnp.bfloat16)
    second_grad = jnp.stack(
        [
            jnp.einsum(
                "btfs,btes->fe",
                second_delta,
                hidden_padded[:, offset : offset + frame_count],
                preferred_element_type=jnp.float32,
            )
            for offset in range(3)
        ]
    )
    delta_padded = pad_second(second_delta)
    hidden_grad = sum(
        (
            jnp.einsum(
                "fe,btfs->btes",
                second_weight[offset],
                delta_padded[:, 2 - offset : 2 - offset + frame_count],
                preferred_element_type=jnp.float32,
            )
            for offset in range(3)
        )
    )
    first_delta = (hidden_grad * leaky_slope(first_pre)).astype(jnp.bfloat16)
    first_grad = jnp.stack(
        [
            jnp.einsum(
                "btes,btps->ep",
                first_delta,
                padded[:, offset : offset + frame_count],
                preferred_element_type=jnp.float32,
            )
            for offset in range(3)
        ]
    )
    first_padded = pad_first(first_delta)
    recon_grad = sum(
        (
            jnp.einsum(
                "ep,btes->btps",
                first_weight[offset],
                first_padded[:, 2 - offset : 2 - offset + frame_count],
                preferred_element_type=jnp.float32,
            )
            for offset in range(3)
        )
    ).astype(jnp.bfloat16)
    return (recon_grad, first_grad, second_grad, head_grad)


def per_device(
    features,
    conv_weight,
    out_weight,
    first_weight,
    second_weight,
    head_weight,
    span_lengths,
    labels,
):
    clip_count, frame_count, channel_count, position_count = features.shape
    slab_count = lax.axis_size("tm")
    total_count = (
        clip_count
        * lax.axis_size("dp")
        * lax.axis_size("group")
        * frame_count
        * slab_count
        * position_count
    )
    loss_scale = float(total_count) ** (-0.5)
    tap_masks = span_masks(span_lengths, lax.axis_index("tm") * frame_count, frame_count)
    earlier_frames = shifted(features[:, frame_count - 2 :], "tm", 1)
    extended = jnp.concatenate([earlier_frames, features], axis=1)
    pre = sum(
        (
            tap_masks[offset][:, :, None, None]
            * jnp.einsum(
                "oi,btis->btos",
                conv_weight[offset],
                extended[:, 2 - offset : 2 - offset + frame_count],
                preferred_element_type=jnp.float32,
            )
            for offset in range(3)
        )
    )
    hidden = (features.astype(jnp.float32) + jax.nn.silu(pre)).astype(jnp.bfloat16)
    recon = jnp.einsum(
        "pc,btcs->btps", out_weight, hidden, preferred_element_type=jnp.float32
    ).astype(jnp.bfloat16)

    def pad_input(values):
        return with_halo(values, (("tm", 1),), 1)

    def pad_hidden(values):
        return with_halo(values, (("tm", 1),), 1)

    def pad_second(values):
        return with_halo(values, (("tm", 1),), 1)

    def pad_first(values):
        return with_halo(values, (("tm", 1),), 1)

    recon_grad, first_grad, second_grad, head_grad = discriminate(
        recon,
        first_weight,
        second_weight,
        head_weight,
        labels,
        loss_scale,
        pad_input,
        pad_hidden,
        pad_second,
        pad_first,
    )
    out_grad = jnp.einsum("btps,btcs->pc", recon_grad, hidden, preferred_element_type=jnp.float32)
    hidden_delta = jnp.einsum(
        "pc,btps->btcs", out_weight, recon_grad, preferred_element_type=jnp.float32
    )
    gating = jax.nn.sigmoid(pre)
    pre_delta = (hidden_delta * gating * (1.0 + pre * (1.0 - gating))).astype(jnp.bfloat16)
    conv_grad = jnp.stack(
        [
            jnp.einsum(
                "btos,btis->oi",
                pre_delta * tap_masks[offset][:, :, None, None].astype(jnp.bfloat16),
                extended[:, 2 - offset : 2 - offset + frame_count],
                preferred_element_type=jnp.float32,
            )
            for offset in range(3)
        ]
    )
    grads = jnp.concatenate(
        [
            conv_grad,
            second_grad,
            jnp.swapaxes(first_grad, 1, 2),
            out_grad.reshape(3, 16, 256),
            jnp.pad(head_grad.reshape(1, 1, 256), ((0, 2), (0, 63), (0, 0))),
        ],
        axis=1,
    )
    summed = all_sum(grads)
    return (
        summed[:, :256],
        summed[:, 560:576].reshape(48, 256),
        jnp.swapaxes(summed[:, 512:560], 1, 2),
        summed[:, 256:512],
        summed[0, 576],
    )


def solution(mesh):
    placed = (
        P(("dp", "group"), "tm", None, None),
        P(),
        P(),
        P(),
        P(),
        P(),
        P(("dp", "group"), None),
        P(("dp", "group")),
    )
    return jax.shard_map(
        per_device, mesh=mesh, in_specs=placed, out_specs=(P(), P(), P(), P(), P()), check_vma=False
    )
```

```python
import functools

import jax
import jax.numpy as jnp
from jax import lax
from jax.experimental import pallas as pl
from jax.experimental.pallas import tpu as pltpu
from jax.sharding import PartitionSpec as P

MESH = pl.DeviceIdType.MESH
F32 = jnp.float32


class Place:
    def __init__(self):
        tm, dp, group = (lax.axis_index(name) for name in ("tm", "dp", "group"))
        self.core = lax.rem(tm, 2)
        self.at = (tm // 2, dp // 2, 2 * group + lax.rem(dp, 2))

    def device(self, x, y, z, core):
        return (2 * x + core, 2 * y + lax.rem(z, 2), z // 2)

    def along(self, axis, step):
        place = list(self.at)
        place[axis] = lax.rem(place[axis] + step, 4)
        return self.device(*place, self.core)

    def other_core(self):
        return self.device(*self.at, 1 - self.core)


class Reducer:
    def __init__(self, place, grads, total, bufs, send_sems, recv_sems):
        self.place, self.grads, self.total = (place, grads, total)
        self.core_in, self.sum1, self.in1, self.sum2, self.in2, self.in3 = bufs
        self.send_sems, self.recv_sems = (send_sems, recv_sems)
        self.rows = grads.shape[1]
        self.sent = []
        self.axes = [tuple((part + i) % 3 for i in range(3)) for part in range(3)]

    def copy(self, src, dst, slot, device):
        return pltpu.make_async_remote_copy(
            src_ref=src,
            dst_ref=dst,
            send_sem=self.send_sems.at[slot],
            recv_sem=self.recv_sems.at[slot],
            device_id=device,
            device_id_type=MESH,
        )

    def start(self, *args):
        copy = self.copy(*args)
        copy.start()
        self.sent.append(copy)

    def lanes(self, core):
        return pl.ds(pl.multiple_of(core * 128, 128), 128)

    def block(self, index, size):
        return pl.ds(pl.multiple_of(index * size, size), size)

    def slot(self, stage, part, step):
        return 3 + (stage * 3 + part) * 3 + step - 1

    def core_send(self, part):
        place = self.place
        src = self.grads.at[part, :, self.lanes(1 - place.core)]
        self.start(src, self.core_in.at[part], part, place.other_core())

    def core_sum(self, part):
        place = self.place
        self.copy(self.core_in.at[part], self.core_in.at[part], part, place.other_core()).wait_recv()
        self.sum1[part] = self.grads[part, :, self.lanes(place.core)] + self.core_in[part]

    def scatter_send(self, part, level):
        axis = self.axes[part][level]
        source, landing = ((self.sum1, self.in1), (self.sum2, self.in2))[level]
        size = landing.shape[2]
        for step in (1, 2, 3):
            target = lax.rem(self.place.at[axis] + step, 4)
            self.start(
                source.at[part, self.block(target, size)],
                landing.at[part, step - 1],
                self.slot(level, part, step),
                self.place.along(axis, step),
            )

    def scatter_sum(self, part, level):
        axis = self.axes[part][level]
        source, landing = ((self.sum1, self.in1), (self.sum2, self.in2))[level]
        size = landing.shape[2]
        for step in (1, 2, 3):
            here = landing.at[part, step - 1]
            self.copy(here, here, self.slot(level, part, step), self.place.along(axis, step)).wait_recv()
        result = source[part, self.block(self.place.at[axis], size)]
        for step in (1, 2, 3):
            result = result + landing[part, step - 1]
        if level == 0:
            self.sum2[part] = result
        else:
            self.in3[part, self.place.at[self.axes[part][2]]] = result

    def swap_send(self, part):
        axis = self.axes[part][2]
        here = self.in3.at[part, self.place.at[axis]]
        for step in (1, 2, 3):
            self.start(here, here, self.slot(2, part, step), self.place.along(axis, step))

    def rows_of(self, part, level):
        first = self.place.at[self.axes[part][0]]
        if level == 0:
            return self.block(first, self.rows // 4)
        return self.block(4 * first + self.place.at[self.axes[part][1]], self.rows // 16)

    def swap_sum(self, part):
        axis = self.axes[part][2]
        for step in (1, 2, 3):
            here = self.in3.at[part, step]
            self.copy(here, here, self.slot(2, part, step), self.place.along(axis, step)).wait_recv()
        result = (self.in3[part, 0] + self.in3[part, 1]) + (self.in3[part, 2] + self.in3[part, 3])
        self.total[part, self.rows_of(part, 1), self.lanes(self.place.core)] = result.astype(self.total.dtype)

    def gather_send(self, part, level):
        axis = self.axes[part][level]
        here = self.total.at[part, self.rows_of(part, level), self.lanes(self.place.core)]
        for step in (1, 2, 3):
            self.start(here, here, self.slot(4 - level, part, step), self.place.along(axis, step))

    def gather_wait(self, part, level):
        axis = self.axes[part][level]
        here = self.total.at[part, self.rows_of(part, level), self.lanes(self.place.core)]
        for step in (1, 2, 3):
            self.copy(here, here, self.slot(4 - level, part, step), self.place.along(axis, step)).wait_recv()

    def back_send(self, part):
        here = self.total.at[part, :, self.lanes(self.place.core)]
        self.start(here, here, 48 + part, self.place.other_core())

    def back_wait(self, part):
        here = self.total.at[part, :, self.lanes(1 - self.place.core)]
        self.copy(here, here, 48 + part, self.place.other_core()).wait_recv()

    def steps(self):
        def each(*calls):
            def run():
                for part in range(3):
                    for call, *level in calls:
                        call(part, *level)

            return run

        return [
            each((self.core_send,)),
            each((self.core_sum,), (self.scatter_send, 0)),
            each((self.scatter_sum, 0), (self.scatter_send, 1)),
            each((self.scatter_sum, 1), (self.swap_send,)),
            each((self.swap_sum,), (self.gather_send, 1)),
            each((self.gather_wait, 1), (self.gather_send, 0)),
            each((self.gather_wait, 0), (self.back_send,)),
            each((self.back_wait,)),
        ]

    def finish(self):
        for copy in self.sent:
            copy.wait_send()


N_SLOTS = 51


def reduce_scratch(rows):
    return [
        pltpu.VMEM((3, rows, 128), F32),
        pltpu.VMEM((3, rows, 128), F32),
        pltpu.VMEM((3, 3, rows // 4, 128), F32),
        pltpu.VMEM((3, rows // 4, 128), F32),
        pltpu.VMEM((3, 3, rows // 16, 128), F32),
        pltpu.VMEM((3, 4, rows // 16, 128), F32),
    ]


SC = 256
WIDTH = 1024
NCH = WIDTH // SC
MIB = 1024 * 1024


def dot(a, b):
    return jnp.dot(a, b, preferred_element_type=F32)


def dot_nt(a, b):
    return lax.dot_general(a, b, (((1,), (1,)), ((), ())), preferred_element_type=F32)


def rows_at(frame, height, count=1):
    start = frame * height
    return pl.ds(start if isinstance(start, int) else pl.multiple_of(start, height), height * count)


def frame_loop(low, high, group, body):
    count = (high - low) // group
    if count == 1:
        for frame in range(low, high):
            body(frame)
        return

    def step(index, carry):
        for offset in range(group):
            body(low + index * group + offset)
        return carry

    lax.fori_loop(0, count, step, 0)


def block_kernel(
    loss_scale,
    spans, labels, feat, cw, ow, owt, fw, fwt, sw, swt, head,
    total1, total2,
    frames, hidden, slopes, recon, disc, second, first, parts, rgrad, masked,
    acc_conv, acc_second, acc_first, acc_out, acc_head, grads1, grads2,
    own_sem, core_send, core_recv, halo_send, halo_recv, low_send, low_recv, high_send, high_recv,
    send1, recv1, send2, recv2, *bufs,
):
    place = Place()
    x, y, z = place.at
    core = place.core
    clip_start, clip_end = x == 0, x == 3
    inner_low, inner_high = x > 0, x < 3

    def cols(chunk, base=0):
        return pl.ds(pl.multiple_of(base + chunk * SC, SC), SC)

    def own_copy(chunk):
        return pltpu.make_async_copy(
            feat.at[:, cols(chunk, core * WIDTH)],
            frames.at[rows_at(2 + 4 * core, 256, 4), cols(chunk)],
            own_sem.at[chunk],
        )

    def remote(src, dst, send, recv, device):
        return pltpu.make_async_remote_copy(
            src_ref=src, dst_ref=dst, send_sem=send, recv_sem=recv, device_id=device, device_id_type=MESH
        )

    def core_copy(chunk):
        return remote(
            feat.at[:, cols(chunk, (1 - core) * WIDTH)],
            frames.at[rows_at(2 + 4 * core, 256, 4), cols(chunk)],
            core_send.at[chunk],
            core_recv.at[chunk],
            place.other_core(),
        )

    def halo_copy(chunk, target):
        return remote(
            feat.at[512:1024, cols(chunk, target * WIDTH)],
            frames.at[0:512, cols(chunk)],
            halo_send.at[chunk, target],
            halo_recv.at[chunk],
            place.device(x + 1, y, z, target),
        )

    def low_copy(chunk):
        return remote(
            recon.at[384:576, cols(chunk)],
            recon.at[0:192, cols(chunk)],
            low_send.at[chunk],
            low_recv.at[chunk],
            place.device(x + 1, y, z, core),
        )

    def high_copy(chunk):
        return remote(
            recon.at[192:384, cols(chunk)],
            recon.at[576:768, cols(chunk)],
            high_send.at[chunk],
            high_recv.at[chunk],
            place.device(x - 1, y, z, core),
        )

    for chunk in range(NCH):
        own_copy(chunk).start()

    barrier = pltpu.get_barrier_semaphore()
    partners = [place.other_core()] + [place.along(axis, step) for axis in range(3) for step in (1, 2, 3)]
    partners += [place.device(lax.rem(x + step, 4), y, z, 1 - core) for step in (1, 3)]
    for device in partners:
        pl.semaphore_signal(barrier, inc=1, device_id=device, device_id_type=MESH)
    pl.semaphore_wait(barrier, len(partners))

    for chunk in range(NCH):
        core_copy(chunk).start()

    @pl.when((core == 1) & inner_high)
    def _():
        for chunk in range(NCH):
            for target in (0, 1):
                halo_copy(chunk, target).start()

    @pl.when(clip_start)
    def _():
        frames[0:512] = jnp.zeros((512, WIDTH), jnp.bfloat16)
        recon[0:192] = jnp.zeros((192, WIDTH), jnp.bfloat16)

    @pl.when(clip_end)
    def _():
        recon[576:768] = jnp.zeros((192, WIDTH), jnp.bfloat16)

    ends = []
    for span in range(4):
        ends.append(spans[0, span] + (ends[-1] if ends else 0))

    def span_of(frame):
        return sum((frame >= end).astype(jnp.int32) for end in ends)

    def tap_mask(local, tap):
        frame = 8 * x + local
        same = (span_of(frame) == span_of(frame - tap)) & (frame >= tap)
        return jnp.where(same, 1.0, 0.0).astype(F32)

    def valid(local):
        frame = 8 * x + local
        return jnp.where((frame >= 0) & (frame < 32), 1.0, 0.0).astype(F32)

    def mask_weights(local, carry):
        rows = rows_at(local, 256)
        for place_of, tap in ((0, 2), (1, 1)):
            lanes = slice(256 * place_of, 256 * place_of + 256)
            weight = cw[:, lanes].astype(F32) * tap_mask(local, tap)
            masked[rows, lanes] = weight.astype(jnp.bfloat16)
        masked[rows, 512:768] = cw[:, 512:768]
        return carry

    lax.fori_loop(0, 8, mask_weights, 0)
    for acc in (acc_conv, acc_second, acc_first, acc_out, acc_head):
        acc[...] = jnp.zeros_like(acc)

    sign = (2 * labels[0] - 1).astype(F32)

    def decode(local, where):
        pre = dot(masked[rows_at(local, 256)], frames[rows_at(local, 256, 3), where])
        gate = 0.5 * jnp.tanh(0.5 * pre) + 0.5
        silu = pre * gate
        value = (frames[rows_at(local + 2, 256), where].astype(F32) + silu).astype(jnp.bfloat16)
        hidden[rows_at(local, 256), where] = value
        slopes[rows_at(local, 256), where] = gate + silu * (1.0 - gate)
        recon[rows_at(local + 4, 48), where] = dot(ow[...], value).astype(jnp.bfloat16)

    def decode_inner(chunk, carry):
        own_copy(chunk).wait()
        core_copy(chunk).wait_recv()
        frame_loop(2, 8, 3, lambda local: decode(local, cols(chunk)))
        return carry

    def decode_halo(chunk):
        @pl.when(inner_low)
        def _():
            halo_copy(chunk, 0).wait_recv()

        decode(0, cols(chunk))
        decode(1, cols(chunk))

        @pl.when(inner_high)
        def _():
            low_copy(chunk).start()

        @pl.when(inner_low)
        def _():
            high_copy(chunk).start()

    def first_layer(local, where):
        pre = dot(fw[...], recon[rows_at(local + 3, 48, 3), where])
        on = valid(local)
        value = pre * jnp.where(pre > 0, on, 0.2 * on)
        disc[rows_at(local + 3, 256)] = value.astype(jnp.bfloat16)

    def second_layer(local, own):
        pre = dot(sw[...], disc[rows_at(local + 2, 256, 3)])
        act = jnp.maximum(pre, 0.2 * pre)
        logits = jnp.sum(act * head[...], axis=0, keepdims=True)
        grad = (-sign * loss_scale * valid(local)) / (1.0 + jnp.exp(sign * logits))
        if own:
            term = act * grad
            acc_head[...] += sum(term[:, i : i + 128] for i in range(0, SC, 128))
        delta = head[...] * grad
        second[rows_at(local + 2, 256)] = jnp.where(pre > 0, delta, 0.2 * delta).astype(jnp.bfloat16)

    def first_back(local):
        back = dot(swt[...], second[rows_at(local + 1, 256, 3)])
        on = valid(local)
        slope = jnp.where(disc[rows_at(local + 3, 256)].astype(F32) > 0, on, 0.2 * on)
        value = (back * slope).astype(jnp.bfloat16)
        first[rows_at(local + 1, 256)] = value
        parts[rows_at(local + 1, 144)] = dot(fwt[...], value)

    def recon_back(local, where):
        total = (
            parts[pl.ds((local + 2) * 144, 48)]
            + parts[pl.ds((local + 1) * 144 + 48, 48)]
            + parts[pl.ds(local * 144 + 96, 48)]
        )
        rgrad[rows_at(local, 48), where] = total.astype(jnp.bfloat16)

    def wide(ref, starts, count, where=slice(None)):
        return jnp.concatenate([ref[start : start + count, where] for start in starts], axis=1)

    def weight_grads(where):
        own = range(8)
        acc_second[...] += dot_nt(
            wide(disc, [(t + 2) * 256 for t in own], 768), wide(second, [(t + 2) * 256 for t in own], 256)
        )
        acc_first[...] += dot_nt(
            wide(recon, [(t + 3) * 48 for t in own], 144, where), wide(first, [(t + 1) * 256 for t in own], 256)
        )
        acc_out[...] += dot_nt(
            wide(rgrad, [t * 48 for t in own], 48, where), wide(hidden, [t * 256 for t in own], 256, where)
        )

    lax.fori_loop(0, NCH - 1, decode_inner, 0)
    decode_halo(0)
    decode_inner(NCH - 1, 0)

    def chunk_step(chunk, carry):
        where = cols(chunk)

        @pl.when(inner_low)
        def _():
            low_copy(chunk).wait_recv()

        @pl.when(inner_high)
        def _():
            high_copy(chunk).wait_recv()

        frame_loop(-3, 11, 7, lambda local: first_layer(local, where))
        frame_loop(-2, 0, 2, lambda local: second_layer(local, False))
        frame_loop(0, 8, 4, lambda local: second_layer(local, True))
        frame_loop(8, 10, 2, lambda local: second_layer(local, False))
        frame_loop(-1, 9, 5, first_back)
        for local in range(8):
            recon_back(local, where)

        @pl.when(chunk < NCH - 1)
        def _():
            decode_halo(chunk + 1)

        weight_grads(where)
        return carry

    lax.fori_loop(0, NCH, chunk_step, 0)

    for part in range(3):
        grads1[part, 0:256] = acc_second[256 * part : 256 * part + 256].T
        grads1[part, 256:304] = acc_first[48 * part : 48 * part + 48]
        grads1[part, 304:320] = acc_out[16 * part : 16 * part + 16]
        grads1[part, 320:384] = jnp.zeros((64, 256), F32)
    grads1[0, 320:328] = jnp.broadcast_to(jnp.sum(acc_head[...].T, axis=0, keepdims=True), (8, 256))

    reduce1 = Reducer(place, grads1, total1, bufs[:6], send1, recv1)
    reduce2 = Reducer(place, grads2, total2, bufs[6:], send2, recv2)
    steps1, steps2 = reduce1.steps(), reduce2.steps()

    def conv_back(local):
        back = dot(owt[...], rgrad[rows_at(local, 48)])
        delta = (back * slopes[rows_at(local, 256)]).astype(jnp.bfloat16)
        result = dot_nt(frames[rows_at(local, 256, 3)], delta)
        for block, tap in ((0, 2), (1, 1), (2, 0)):
            rows = slice(256 * block, 256 * block + 256)
            acc_conv[rows] += result[rows] * tap_mask(local, tap)

    steps1[0]()
    for pair in range(4):
        lax.fori_loop(2 * pair, 2 * pair + 2, lambda local, carry: (conv_back(local), carry)[1], 0)
        if pair < 3:
            steps1[pair + 1]()
    for tap in range(3):
        grads2[tap] = acc_conv[256 * (2 - tap) : 256 * (2 - tap) + 256].T
    steps2[0]()
    for index in range(4, 8):
        steps1[index]()
        steps2[index - 3]()
    for index in range(5, 8):
        steps2[index]()

    reduce1.finish()
    reduce2.finish()
    for chunk in range(NCH):
        core_copy(chunk).wait_send()

        @pl.when((core == 1) & inner_high)
        def _():
            halo_copy(chunk, 0).wait_send()
            halo_copy(chunk, 1).wait_send()

        @pl.when(inner_high)
        def _():
            low_copy(chunk).wait_send()

        @pl.when(inner_low)
        def _():
            high_copy(chunk).wait_send()


def per_device(
    features, conv_weight, out_weight, first_weight, second_weight, head_weight, span_lengths, labels
):
    clips, frame_count, channels, positions = features.shape
    total_count = (
        clips * lax.axis_size("dp") * lax.axis_size("group") * frame_count * lax.axis_size("tm") * positions
    )
    loss_scale = float(total_count) ** (-0.5)
    bf16 = jnp.bfloat16
    operands = (
        span_lengths,
        labels,
        features.reshape(frame_count * channels, positions),
        jnp.concatenate([conv_weight[2], conv_weight[1], conv_weight[0]], axis=1),
        out_weight,
        out_weight.T,
        jnp.concatenate([first_weight[0], first_weight[1], first_weight[2]], axis=1),
        jnp.swapaxes(first_weight, 1, 2).reshape(144, 256),
        jnp.concatenate([second_weight[0], second_weight[1], second_weight[2]], axis=1),
        jnp.concatenate([second_weight[2].T, second_weight[1].T, second_weight[0].T], axis=1),
        jnp.broadcast_to(head_weight.astype(F32)[:, None], (256, SC)),
    )
    smem, vmem = pl.BlockSpec(memory_space=pltpu.SMEM), pl.BlockSpec(memory_space=pltpu.VMEM)
    dma = pltpu.SemaphoreType.DMA
    total1, total2 = pl.pallas_call(
        functools.partial(block_kernel, loss_scale),
        out_shape=(
            jax.ShapeDtypeStruct((3, 384, 256), F32),
            jax.ShapeDtypeStruct((3, 256, 256), F32),
        ),
        in_specs=[smem, smem, pl.BlockSpec(memory_space=pl.ANY)] + [vmem] * 8,
        out_specs=(vmem, vmem),
        scratch_shapes=[
            pltpu.VMEM((2560, WIDTH), bf16),
            pltpu.VMEM((2048, WIDTH), bf16),
            pltpu.VMEM((2048, WIDTH), F32),
            pltpu.VMEM((768, WIDTH), bf16),
            pltpu.VMEM((14 * 256, SC), bf16),
            pltpu.VMEM((12 * 256, SC), bf16),
            pltpu.VMEM((10 * 256, SC), bf16),
            pltpu.VMEM((10 * 144, SC), F32),
            pltpu.VMEM((8 * 48, WIDTH), bf16),
            pltpu.VMEM((2048, 768), bf16),
            pltpu.VMEM((768, 256), F32),
            pltpu.VMEM((768, 256), F32),
            pltpu.VMEM((144, 256), F32),
            pltpu.VMEM((48, 256), F32),
            pltpu.VMEM((256, 128), F32),
            pltpu.VMEM((3, 384, 256), F32),
            pltpu.VMEM((3, 256, 256), F32),
            dma((NCH,)),
            dma((NCH,)),
            dma((NCH,)),
            dma((NCH, 2)),
            dma((NCH,)),
            dma((NCH,)),
            dma((NCH,)),
            dma((NCH,)),
            dma((NCH,)),
            dma((N_SLOTS,)),
            dma((N_SLOTS,)),
            dma((N_SLOTS,)),
            dma((N_SLOTS,)),
        ]
        + reduce_scratch(384)
        + reduce_scratch(256),
        compiler_params=pltpu.CompilerParams(
            collective_id=0, has_side_effects=True, vmem_limit_bytes=56 * MIB
        ),
    )(*operands)
    return (
        total2,
        total1[:, 304:320].reshape(48, 256),
        jnp.swapaxes(total1[:, 256:304], 1, 2),
        total1[:, 0:256],
        total1[0, 320],
    )


def solution(mesh):
    placed = (
        P(("dp", "group"), "tm", None, None),
        P(),
        P(),
        P(),
        P(),
        P(),
        P(("dp", "group"), None),
        P(("dp", "group")),
    )
    return jax.shard_map(
        per_device, mesh=mesh, in_specs=placed, out_specs=(P(), P(), P(), P(), P()), check_vma=False
    )
```

```python
import functools

import jax
import jax.numpy as jnp
from jax import lax
from jax.experimental import pallas as pl
from jax.experimental.pallas import tpu as pltpu
from jax.sharding import PartitionSpec as P

MESH = pl.DeviceIdType.MESH
F32 = jnp.float32


class Place:
    def __init__(self):
        tm, dp, group = (lax.axis_index(name) for name in ("tm", "dp", "group"))
        self.core = lax.rem(tm, 2)
        self.at = (tm // 2, dp // 2, 2 * group + lax.rem(dp, 2))

    def device(self, x, y, z, core):
        return (2 * x + core, 2 * y + lax.rem(z, 2), z // 2)

    def along(self, axis, step):
        place = list(self.at)
        place[axis] = lax.rem(place[axis] + step, 4)
        return self.device(*place, self.core)

    def other_core(self):
        return self.device(*self.at, 1 - self.core)


class Reducer:
    def __init__(self, place, grads, total, bufs, send_sems, recv_sems):
        self.place, self.grads, self.total = (place, grads, total)
        self.core_in, self.sum1, self.in1, self.sum2, self.in2, self.in3 = bufs
        self.send_sems, self.recv_sems = (send_sems, recv_sems)
        self.rows = grads.shape[1]
        self.sent = []
        self.axes = [tuple((part + i) % 3 for i in range(3)) for part in range(3)]

    def copy(self, src, dst, slot, device):
        return pltpu.make_async_remote_copy(
            src_ref=src,
            dst_ref=dst,
            send_sem=self.send_sems.at[slot],
            recv_sem=self.recv_sems.at[slot],
            device_id=device,
            device_id_type=MESH,
        )

    def start(self, *args):
        copy = self.copy(*args)
        copy.start()
        self.sent.append(copy)

    def lanes(self, core):
        return pl.ds(pl.multiple_of(core * 128, 128), 128)

    def block(self, index, size):
        return pl.ds(pl.multiple_of(index * size, size), size)

    def slot(self, stage, part, step):
        return 3 + (stage * 3 + part) * 3 + step - 1

    def core_send(self, part):
        place = self.place
        src = self.grads.at[part, :, self.lanes(1 - place.core)]
        self.start(src, self.core_in.at[part], part, place.other_core())

    def core_sum(self, part):
        place = self.place
        self.copy(self.core_in.at[part], self.core_in.at[part], part, place.other_core()).wait_recv()
        self.sum1[part] = self.grads[part, :, self.lanes(place.core)] + self.core_in[part]

    def scatter_send(self, part, level):
        axis = self.axes[part][level]
        source, landing = ((self.sum1, self.in1), (self.sum2, self.in2))[level]
        size = landing.shape[2]
        for step in (1, 2, 3):
            target = lax.rem(self.place.at[axis] + step, 4)
            self.start(
                source.at[part, self.block(target, size)],
                landing.at[part, step - 1],
                self.slot(level, part, step),
                self.place.along(axis, step),
            )

    def scatter_sum(self, part, level):
        axis = self.axes[part][level]
        source, landing = ((self.sum1, self.in1), (self.sum2, self.in2))[level]
        size = landing.shape[2]
        for step in (1, 2, 3):
            here = landing.at[part, step - 1]
            self.copy(here, here, self.slot(level, part, step), self.place.along(axis, step)).wait_recv()
        result = source[part, self.block(self.place.at[axis], size)]
        for step in (1, 2, 3):
            result = result + landing[part, step - 1]
        if level == 0:
            self.sum2[part] = result
        else:
            self.in3[part, self.place.at[self.axes[part][2]]] = result

    def swap_send(self, part):
        axis = self.axes[part][2]
        here = self.in3.at[part, self.place.at[axis]]
        for step in (1, 2, 3):
            self.start(here, here, self.slot(2, part, step), self.place.along(axis, step))

    def rows_of(self, part, level):
        first = self.place.at[self.axes[part][0]]
        if level == 0:
            return self.block(first, self.rows // 4)
        return self.block(4 * first + self.place.at[self.axes[part][1]], self.rows // 16)

    def swap_sum(self, part):
        axis = self.axes[part][2]
        for step in (1, 2, 3):
            here = self.in3.at[part, step]
            self.copy(here, here, self.slot(2, part, step), self.place.along(axis, step)).wait_recv()
        result = (self.in3[part, 0] + self.in3[part, 1]) + (self.in3[part, 2] + self.in3[part, 3])
        self.total[part, self.rows_of(part, 1), self.lanes(self.place.core)] = result.astype(self.total.dtype)

    def gather_send(self, part, level):
        axis = self.axes[part][level]
        here = self.total.at[part, self.rows_of(part, level), self.lanes(self.place.core)]
        for step in (1, 2, 3):
            self.start(here, here, self.slot(4 - level, part, step), self.place.along(axis, step))

    def gather_wait(self, part, level):
        axis = self.axes[part][level]
        here = self.total.at[part, self.rows_of(part, level), self.lanes(self.place.core)]
        for step in (1, 2, 3):
            self.copy(here, here, self.slot(4 - level, part, step), self.place.along(axis, step)).wait_recv()

    def back_send(self, part):
        here = self.total.at[part, :, self.lanes(self.place.core)]
        self.start(here, here, 48 + part, self.place.other_core())

    def back_wait(self, part):
        here = self.total.at[part, :, self.lanes(1 - self.place.core)]
        self.copy(here, here, 48 + part, self.place.other_core()).wait_recv()

    def steps(self):
        def each(*calls):
            def run():
                for part in range(3):
                    for call, *level in calls:
                        call(part, *level)

            return run

        return [
            each((self.core_send,)),
            each((self.core_sum,), (self.scatter_send, 0)),
            each((self.scatter_sum, 0), (self.scatter_send, 1)),
            each((self.scatter_sum, 1), (self.swap_send,)),
            each((self.swap_sum,), (self.gather_send, 1)),
            each((self.gather_wait, 1), (self.gather_send, 0)),
            each((self.gather_wait, 0), (self.back_send,)),
            each((self.back_wait,)),
        ]

    def finish(self):
        for copy in self.sent:
            copy.wait_send()


N_SLOTS = 51


def reduce_scratch(rows):
    return [
        pltpu.VMEM((3, rows, 128), F32),
        pltpu.VMEM((3, rows, 128), F32),
        pltpu.VMEM((3, 3, rows // 4, 128), F32),
        pltpu.VMEM((3, rows // 4, 128), F32),
        pltpu.VMEM((3, 3, rows // 16, 128), F32),
        pltpu.VMEM((3, 4, rows // 16, 128), F32),
    ]


SC = 512
WIDTH = 1024
NCH = WIDTH // SC
MIB = 1024 * 1024


def dot(a, b):
    return jnp.dot(a, b, preferred_element_type=F32)


def dot_nt(a, b):
    return lax.dot_general(a, b, (((1,), (1,)), ((), ())), preferred_element_type=F32)


def rows_at(frame, height, count=1):
    start = frame * height
    return pl.ds(start if isinstance(start, int) else pl.multiple_of(start, height), height * count)


def block_kernel(
    loss_scale,
    spans, labels, feat, conv_w, ow, fwt, second_w, head_w,
    conv_out, out_out, first_out, second_out, head_out,
    owt, fw, sw, swt, head, total1, total2,
    frames, hidden, slopes, recon, disc, second, first, parts, rgrad, masked,
    acc_conv, acc_second, acc_first, acc_out, acc_head, grads1, grads2,
    own_sem, core_send, core_recv, halo_send, halo_recv, low_send, low_recv, high_send, high_recv,
    send1, recv1, send2, recv2, *bufs,
):
    place = Place()
    x, y, z = place.at
    core = place.core
    clip_start, clip_end = x == 0, x == 3
    inner_low, inner_high = x > 0, x < 3

    def cols(chunk, base=0):
        return pl.ds(pl.multiple_of(base + chunk * SC, SC), SC)

    def own_copy(chunk):
        return pltpu.make_async_copy(
            feat.at[:, cols(chunk, core * WIDTH)],
            frames.at[rows_at(2 + 4 * core, 256, 4), cols(chunk)],
            own_sem.at[chunk],
        )

    def remote(src, dst, send, recv, device):
        return pltpu.make_async_remote_copy(
            src_ref=src, dst_ref=dst, send_sem=send, recv_sem=recv, device_id=device, device_id_type=MESH
        )

    def core_copy(chunk):
        return remote(
            feat.at[:, cols(chunk, (1 - core) * WIDTH)],
            frames.at[rows_at(2 + 4 * core, 256, 4), cols(chunk)],
            core_send.at[chunk],
            core_recv.at[chunk],
            place.other_core(),
        )

    def halo_copy(chunk, target):
        return remote(
            feat.at[512:1024, cols(chunk, target * WIDTH)],
            frames.at[0:512, cols(chunk)],
            halo_send.at[chunk, target],
            halo_recv.at[chunk],
            place.device(x + 1, y, z, target),
        )

    def low_copy(chunk):
        return remote(
            recon.at[384:576, cols(chunk)],
            recon.at[0:192, cols(chunk)],
            low_send.at[chunk],
            low_recv.at[chunk],
            place.device(x + 1, y, z, core),
        )

    def high_copy(chunk):
        return remote(
            recon.at[192:384, cols(chunk)],
            recon.at[576:768, cols(chunk)],
            high_send.at[chunk],
            high_recv.at[chunk],
            place.device(x - 1, y, z, core),
        )

    for chunk in range(NCH):
        own_copy(chunk).start()

    barrier = pltpu.get_barrier_semaphore()
    partners = [place.other_core()] + [place.along(axis, step) for axis in range(3) for step in (1, 2, 3)]
    partners += [place.device(lax.rem(x + step, 4), y, z, 1 - core) for step in (1, 3)]
    for device in partners:
        pl.semaphore_signal(barrier, inc=1, device_id=device, device_id_type=MESH)
    pl.semaphore_wait(barrier, len(partners))

    for chunk in range(NCH):
        core_copy(chunk).start()

    @pl.when((core == 1) & inner_high)
    def _():
        for chunk in range(NCH):
            for target in (0, 1):
                halo_copy(chunk, target).start()

    @pl.when(clip_start)
    def _():
        frames[0:512] = jnp.zeros((512, WIDTH), jnp.bfloat16)
        recon[0:192] = jnp.zeros((192, WIDTH), jnp.bfloat16)

    @pl.when(clip_end)
    def _():
        recon[576:768] = jnp.zeros((192, WIDTH), jnp.bfloat16)

    ends = []
    for span in range(4):
        ends.append(spans[0, span] + (ends[-1] if ends else 0))

    def span_of(frame):
        return sum((frame >= end).astype(jnp.int32) for end in ends)

    def tap_mask(local, tap):
        frame = 8 * x + local
        same = (span_of(frame) == span_of(frame - tap)) & (frame >= tap)
        return jnp.where(same, 1.0, 0.0).astype(F32)

    def valid(local):
        frame = 8 * x + local
        return jnp.where((frame >= 0) & (frame < 32), 1.0, 0.0).astype(F32)

    def mask_weights(local, carry):
        rows = rows_at(local, 256)
        for block, tap in ((0, 2), (1, 1)):
            weight = conv_w[tap].astype(F32) * tap_mask(local, tap)
            masked[rows, 256 * block : 256 * block + 256] = weight.astype(jnp.bfloat16)
        masked[rows, 512:768] = conv_w[0]
        return carry

    def place_weights():
        row, column = (lax.broadcasted_iota(jnp.int32, (256, 256), axis) for axis in (0, 1))
        same = jnp.where(row == column, 1.0, 0.0).astype(jnp.bfloat16)
        owt[...] = dot_nt(same, ow[...]).astype(jnp.bfloat16)
        fw[...] = dot_nt(same, fwt[...]).astype(jnp.bfloat16)
        for tap in range(3):
            sw[:, 256 * tap : 256 * tap + 256] = second_w[tap]
            turned = dot_nt(same, second_w[tap]).astype(jnp.bfloat16)
            swt[:, 512 - 256 * tap : 768 - 256 * tap] = turned
        row = jnp.broadcast_to(head_w[...].astype(F32), (256, 256)).astype(jnp.bfloat16)
        column = dot_nt(same, row)
        head[...] = jnp.concatenate([column] * (SC // 256), axis=1)

    lax.fori_loop(0, 8, mask_weights, 0)
    place_weights()
    for acc in (acc_conv, acc_second, acc_first, acc_out, acc_head):
        acc[...] = jnp.zeros_like(acc)

    sign = (2 * labels[0] - 1).astype(F32)

    def decode(local, where):
        pre = dot(masked[rows_at(local, 256)], frames[rows_at(local, 256, 3), where])
        gate = 0.5 * jnp.tanh(0.5 * pre) + 0.5
        silu = pre * gate
        value = (frames[rows_at(local + 2, 256), where].astype(F32) + silu).astype(jnp.bfloat16)
        hidden[rows_at(local, 256), where] = value
        slopes[rows_at(local, 256), where] = gate + silu * (1.0 - gate)
        recon[rows_at(local + 4, 48), where] = dot(ow[...], value).astype(jnp.bfloat16)

    def decode_inner(chunk):
        own_copy(chunk).wait()
        core_copy(chunk).wait_recv()
        for local in range(2, 8):
            decode(local, cols(chunk))

    def decode_halo(chunk):
        @pl.when(inner_low)
        def _():
            halo_copy(chunk, 0).wait_recv()

        decode(0, cols(chunk))
        decode(1, cols(chunk))

        @pl.when(inner_high)
        def _():
            low_copy(chunk).start()

        @pl.when(inner_low)
        def _():
            high_copy(chunk).start()

    def first_layer(local, where):
        pre = dot(fw[...], recon[rows_at(local + 3, 48, 3), where])
        on = valid(local)
        value = pre * jnp.where(pre > 0, on, 0.2 * on)
        disc[rows_at(local + 3, 256)] = value.astype(jnp.bfloat16)

    def second_layer(local, own):
        pre = dot(sw[...], disc[rows_at(local + 2, 256, 3)])
        act = jnp.maximum(pre, 0.2 * pre)
        logits = jnp.sum(act * head[...], axis=0, keepdims=True)
        grad = (-sign * loss_scale * valid(local)) / (1.0 + jnp.exp(sign * logits))
        if own:
            term = act * grad
            acc_head[...] += sum(term[:, i : i + 128] for i in range(0, SC, 128))
        delta = head[...] * grad
        second[rows_at(local + 2, 256)] = jnp.where(pre > 0, delta, 0.2 * delta).astype(jnp.bfloat16)

    def first_back(local):
        back = dot(swt[...], second[rows_at(local + 1, 256, 3)])
        on = valid(local)
        slope = jnp.where(disc[rows_at(local + 3, 256)].astype(F32) > 0, on, 0.2 * on)
        value = (back * slope).astype(jnp.bfloat16)
        first[rows_at(local + 1, 256)] = value
        parts[rows_at(local + 1, 144)] = dot(fwt[...], value)

    def recon_back(local, where):
        total = (
            parts[pl.ds((local + 2) * 144, 48)]
            + parts[pl.ds((local + 1) * 144 + 48, 48)]
            + parts[pl.ds(local * 144 + 96, 48)]
        )
        rgrad[rows_at(local, 48), where] = total.astype(jnp.bfloat16)

    def wide(ref, starts, count, where=slice(None)):
        return jnp.concatenate([ref[start : start + count, where] for start in starts], axis=1)

    def weight_grads(where):
        own = range(8)
        acc_second[...] += dot_nt(
            wide(disc, [(t + 2) * 256 for t in own], 768), wide(second, [(t + 2) * 256 for t in own], 256)
        )
        acc_first[...] += dot_nt(
            wide(recon, [(t + 3) * 48 for t in own], 144, where), wide(first, [(t + 1) * 256 for t in own], 256)
        )
        acc_out[...] += dot_nt(
            wide(rgrad, [t * 48 for t in own], 48, where), wide(hidden, [t * 256 for t in own], 256, where)
        )

    for chunk in range(NCH):
        decode_inner(chunk)
    decode_halo(0)

    for chunk in range(NCH):
        where = cols(chunk)

        @pl.when(inner_low)
        def _():
            low_copy(chunk).wait_recv()

        @pl.when(inner_high)
        def _():
            high_copy(chunk).wait_recv()

        for step in range(-3, 14):
            if step < 11:
                first_layer(step, where)
            if -2 <= step - 2 < 10:
                second_layer(step - 2, 0 <= step - 2 < 8)
            if -1 <= step - 4 < 9:
                first_back(step - 4)
            if 0 <= step - 6:
                recon_back(step - 6, where)

        if chunk + 1 < NCH:
            decode_halo(chunk + 1)
        weight_grads(where)

    for part in range(3):
        grads1[part, 0:256] = acc_second[256 * part : 256 * part + 256].T
        grads1[part, 256:304] = acc_first[48 * part : 48 * part + 48]
        grads1[part, 304:320] = acc_out[16 * part : 16 * part + 16]
        grads1[part, 320:384] = jnp.zeros((64, 256), F32)
    grads1[0, 320:328] = jnp.broadcast_to(jnp.sum(acc_head[...].T, axis=0, keepdims=True), (8, 256))

    reduce1 = Reducer(place, grads1, total1, bufs[:6], send1, recv1)
    reduce2 = Reducer(place, grads2, total2, bufs[6:], send2, recv2)
    steps1, steps2 = reduce1.steps(), reduce2.steps()

    def conv_back(local):
        back = dot(owt[...], rgrad[rows_at(local, 48)])
        delta = (back * slopes[rows_at(local, 256)]).astype(jnp.bfloat16)
        result = dot_nt(frames[rows_at(local, 256, 3)], delta)
        for block, tap in ((0, 2), (1, 1), (2, 0)):
            rows = slice(256 * block, 256 * block + 256)
            acc_conv[rows] += result[rows] * tap_mask(local, tap)

    steps1[0]()
    for pair in range(4):
        conv_back(2 * pair)
        conv_back(2 * pair + 1)
        if pair < 3:
            steps1[pair + 1]()
    for tap in range(3):
        grads2[tap] = acc_conv[256 * (2 - tap) : 256 * (2 - tap) + 256].T
    steps2[0]()
    for index in range(4, 8):
        steps1[index]()
        steps2[index - 3]()
    for index in range(5, 8):
        steps2[index]()

    for part in range(3):
        conv_out[part] = total2[part].astype(F32)
        second_out[part] = total1[part, 0:256]
        first_out[part] = total1[part, 256:304]
        out_out[16 * part : 16 * part + 16] = total1[part, 304:320]
    head_out[...] = total1[0, 320:321]

    reduce1.finish()
    reduce2.finish()
    for chunk in range(NCH):
        core_copy(chunk).wait_send()

        @pl.when((core == 1) & inner_high)
        def _():
            halo_copy(chunk, 0).wait_send()
            halo_copy(chunk, 1).wait_send()

        @pl.when(inner_high)
        def _():
            low_copy(chunk).wait_send()

        @pl.when(inner_low)
        def _():
            high_copy(chunk).wait_send()


def per_device(
    features, conv_weight, out_weight, first_weight, second_weight, head_weight, span_lengths, labels
):
    clips, frame_count, channels, positions = features.shape
    total_count = (
        clips * lax.axis_size("dp") * lax.axis_size("group") * frame_count * lax.axis_size("tm") * positions
    )
    loss_scale = float(total_count) ** (-0.5)
    bf16 = jnp.bfloat16
    operands = (
        span_lengths,
        labels,
        features.reshape(frame_count * channels, positions),
        conv_weight,
        out_weight,
        jnp.swapaxes(first_weight, 1, 2).reshape(144, 256),
        second_weight,
        head_weight.reshape(1, 256),
    )
    smem, vmem = pl.BlockSpec(memory_space=pltpu.SMEM), pl.BlockSpec(memory_space=pltpu.VMEM)
    dma = pltpu.SemaphoreType.DMA
    conv, out, first, second, head = pl.pallas_call(
        functools.partial(block_kernel, loss_scale),
        out_shape=(
            jax.ShapeDtypeStruct((3, 256, 256), F32),
            jax.ShapeDtypeStruct((48, 256), F32),
            jax.ShapeDtypeStruct((3, 48, 256), F32),
            jax.ShapeDtypeStruct((3, 256, 256), F32),
            jax.ShapeDtypeStruct((1, 256), F32),
        ),
        in_specs=[smem, smem, pl.BlockSpec(memory_space=pl.ANY)] + [vmem] * 5,
        out_specs=(vmem,) * 5,
        scratch_shapes=[
            pltpu.VMEM((256, 48), bf16),
            pltpu.VMEM((256, 144), bf16),
            pltpu.VMEM((256, 768), bf16),
            pltpu.VMEM((256, 768), bf16),
            pltpu.VMEM((256, SC), F32),
            pltpu.VMEM((3, 384, 256), F32),
            pltpu.VMEM((3, 256, 256), bf16),
            pltpu.VMEM((2560, WIDTH), bf16),
            pltpu.VMEM((2048, WIDTH), bf16),
            pltpu.VMEM((2048, WIDTH), F32),
            pltpu.VMEM((768, WIDTH), bf16),
            pltpu.VMEM((14 * 256, SC), bf16),
            pltpu.VMEM((12 * 256, SC), bf16),
            pltpu.VMEM((10 * 256, SC), bf16),
            pltpu.VMEM((10 * 144, SC), F32),
            pltpu.VMEM((8 * 48, WIDTH), bf16),
            pltpu.VMEM((2048, 768), bf16),
            pltpu.VMEM((768, 256), F32),
            pltpu.VMEM((768, 256), F32),
            pltpu.VMEM((144, 256), F32),
            pltpu.VMEM((48, 256), F32),
            pltpu.VMEM((256, 128), F32),
            pltpu.VMEM((3, 384, 256), F32),
            pltpu.VMEM((3, 256, 256), F32),
            dma((NCH,)),
            dma((NCH,)),
            dma((NCH,)),
            dma((NCH, 2)),
            dma((NCH,)),
            dma((NCH,)),
            dma((NCH,)),
            dma((NCH,)),
            dma((NCH,)),
            dma((N_SLOTS,)),
            dma((N_SLOTS,)),
            dma((N_SLOTS,)),
            dma((N_SLOTS,)),
        ]
        + reduce_scratch(384)
        + reduce_scratch(256),
        compiler_params=pltpu.CompilerParams(
            collective_id=0, has_side_effects=True, vmem_limit_bytes=56 * MIB
        ),
    )(*operands)
    return conv, out, jnp.swapaxes(first, 1, 2), second, head.reshape(256)


def solution(mesh):
    placed = (
        P(("dp", "group"), "tm", None, None),
        P(),
        P(),
        P(),
        P(),
        P(),
        P(("dp", "group"), None),
        P(("dp", "group")),
    )
    return jax.shard_map(
        per_device, mesh=mesh, in_specs=placed, out_specs=(P(), P(), P(), P(), P()), check_vma=False
    )
```

```python
import functools

import jax
import jax.numpy as jnp
from jax import lax
from jax.experimental import pallas as pl
from jax.experimental.pallas import tpu as pltpu
from jax.sharding import PartitionSpec as P

MESH = pl.DeviceIdType.MESH
F32 = jnp.float32


class Place:
    def __init__(self):
        tm, dp, group = (lax.axis_index(name) for name in ("tm", "dp", "group"))
        self.core = lax.rem(tm, 2)
        self.at = (tm // 2, dp // 2, 2 * group + lax.rem(dp, 2))

    def device(self, x, y, z, core):
        return (2 * x + core, 2 * y + lax.rem(z, 2), z // 2)

    def along(self, axis, step):
        place = list(self.at)
        place[axis] = lax.rem(place[axis] + step, 4)
        return self.device(*place, self.core)

    def other_core(self):
        return self.device(*self.at, 1 - self.core)


class Reducer:
    def __init__(self, place, grads, total, bufs, send_sems, recv_sems):
        self.place, self.grads, self.total = (place, grads, total)
        self.core_in, self.sum1, self.in1, self.sum2, self.in2, self.in3 = bufs
        self.send_sems, self.recv_sems = (send_sems, recv_sems)
        self.rows = grads.shape[1]
        self.sent = []
        self.axes = [tuple((part + i) % 3 for i in range(3)) for part in range(3)]

    def copy(self, src, dst, slot, device):
        return pltpu.make_async_remote_copy(
            src_ref=src,
            dst_ref=dst,
            send_sem=self.send_sems.at[slot],
            recv_sem=self.recv_sems.at[slot],
            device_id=device,
            device_id_type=MESH,
        )

    def start(self, *args):
        copy = self.copy(*args)
        copy.start()
        self.sent.append(copy)

    def lanes(self, core):
        return pl.ds(pl.multiple_of(core * 128, 128), 128)

    def block(self, index, size):
        return pl.ds(pl.multiple_of(index * size, size), size)

    def slot(self, stage, part, step):
        return 3 + (stage * 3 + part) * 3 + step - 1

    def core_send(self, part):
        place = self.place
        src = self.grads.at[part, :, self.lanes(1 - place.core)]
        self.start(src, self.core_in.at[part], part, place.other_core())

    def core_sum(self, part):
        place = self.place
        self.copy(self.core_in.at[part], self.core_in.at[part], part, place.other_core()).wait_recv()
        self.sum1[part] = self.grads[part, :, self.lanes(place.core)] + self.core_in[part]

    def scatter_send(self, part, level):
        axis = self.axes[part][level]
        source, landing = ((self.sum1, self.in1), (self.sum2, self.in2))[level]
        size = landing.shape[2]
        for step in (1, 2, 3):
            target = lax.rem(self.place.at[axis] + step, 4)
            self.start(
                source.at[part, self.block(target, size)],
                landing.at[part, step - 1],
                self.slot(level, part, step),
                self.place.along(axis, step),
            )

    def scatter_sum(self, part, level):
        axis = self.axes[part][level]
        source, landing = ((self.sum1, self.in1), (self.sum2, self.in2))[level]
        size = landing.shape[2]
        for step in (1, 2, 3):
            here = landing.at[part, step - 1]
            self.copy(here, here, self.slot(level, part, step), self.place.along(axis, step)).wait_recv()
        result = source[part, self.block(self.place.at[axis], size)]
        for step in (1, 2, 3):
            result = result + landing[part, step - 1]
        if level == 0:
            self.sum2[part] = result
        else:
            self.in3[part, self.place.at[self.axes[part][2]]] = result

    def swap_send(self, part):
        axis = self.axes[part][2]
        here = self.in3.at[part, self.place.at[axis]]
        for step in (1, 2, 3):
            self.start(here, here, self.slot(2, part, step), self.place.along(axis, step))

    def rows_of(self, part, level):
        first = self.place.at[self.axes[part][0]]
        if level == 0:
            return self.block(first, self.rows // 4)
        return self.block(4 * first + self.place.at[self.axes[part][1]], self.rows // 16)

    def swap_sum(self, part):
        axis = self.axes[part][2]
        for step in (1, 2, 3):
            here = self.in3.at[part, step]
            self.copy(here, here, self.slot(2, part, step), self.place.along(axis, step)).wait_recv()
        result = (self.in3[part, 0] + self.in3[part, 1]) + (self.in3[part, 2] + self.in3[part, 3])
        self.total[part, self.rows_of(part, 1), self.lanes(self.place.core)] = result.astype(self.total.dtype)

    def gather_send(self, part, level):
        axis = self.axes[part][level]
        here = self.total.at[part, self.rows_of(part, level), self.lanes(self.place.core)]
        for step in (1, 2, 3):
            self.start(here, here, self.slot(4 - level, part, step), self.place.along(axis, step))

    def gather_wait(self, part, level):
        axis = self.axes[part][level]
        here = self.total.at[part, self.rows_of(part, level), self.lanes(self.place.core)]
        for step in (1, 2, 3):
            self.copy(here, here, self.slot(4 - level, part, step), self.place.along(axis, step)).wait_recv()

    def back_send(self, part):
        here = self.total.at[part, :, self.lanes(self.place.core)]
        self.start(here, here, 48 + part, self.place.other_core())

    def back_wait(self, part):
        here = self.total.at[part, :, self.lanes(1 - self.place.core)]
        self.copy(here, here, 48 + part, self.place.other_core()).wait_recv()

    def steps(self):
        def each(*calls):
            def run():
                for part in range(3):
                    for call, *level in calls:
                        call(part, *level)

            return run

        return [
            each((self.core_send,)),
            each((self.core_sum,), (self.scatter_send, 0)),
            each((self.scatter_sum, 0), (self.scatter_send, 1)),
            each((self.scatter_sum, 1), (self.swap_send,)),
            each((self.swap_sum,), (self.gather_send, 1)),
            each((self.gather_wait, 1), (self.gather_send, 0)),
            each((self.gather_wait, 0), (self.back_send,)),
            each((self.back_wait,)),
        ]

    def finish(self):
        for copy in self.sent:
            copy.wait_send()


N_SLOTS = 51


def reduce_scratch(rows):
    return [
        pltpu.VMEM((3, rows, 128), F32),
        pltpu.VMEM((3, rows, 128), F32),
        pltpu.VMEM((3, 3, rows // 4, 128), F32),
        pltpu.VMEM((3, rows // 4, 128), F32),
        pltpu.VMEM((3, 3, rows // 16, 128), F32),
        pltpu.VMEM((3, 4, rows // 16, 128), F32),
    ]


SC = 512
WIDTH = 1024
NCH = WIDTH // SC
MIB = 1024 * 1024


def dot(a, b):
    return jnp.dot(a, b, preferred_element_type=F32)


def dot_nt(a, b):
    return lax.dot_general(a, b, (((1,), (1,)), ((), ())), preferred_element_type=F32)


def rows_at(frame, height, count=1):
    start = frame * height
    return pl.ds(start if isinstance(start, int) else pl.multiple_of(start, height), height * count)


def finish_kernel(total1, total2, conv_out, out_out, first_out, second_out, head_out):
    for part in range(3):
        conv_out[part] = total2[part].astype(F32)
        second_out[part] = total1[part, 0:256]
        first_out[part] = total1[part, 256:304]
        out_out[16 * part : 16 * part + 16] = total1[part, 304:320]
    head_out[...] = total1[0, 320:321]


def block_kernel(
    loss_scale,
    spans, labels, feat, conv_w, ow, fwt, second_w, head_w,
    total1, total2,
    frames, turned, hidden, slopes, recon, disc, disc_t, second, first, parts, rgrad, conv_t, masked, second_t,
    acc_conv, acc_second, acc_first, acc_out, acc_head, grads1, grads2,
    own_sem, core_send, core_recv, halo_send, halo_recv, low_send, low_recv, high_send, high_recv,
    send1, recv1, send2, recv2, *bufs,
):
    place = Place()
    x, y, z = place.at
    core = place.core
    clip_start, clip_end = x == 0, x == 3
    inner_low, inner_high = x > 0, x < 3

    def cols(chunk, base=0):
        return pl.ds(pl.multiple_of(base + chunk * SC, SC), SC)

    def own_copy(chunk):
        return pltpu.make_async_copy(
            feat.at[:, cols(chunk, core * WIDTH)],
            frames.at[rows_at(2 + 4 * core, 256, 4), cols(chunk)],
            own_sem.at[chunk],
        )

    def remote(src, dst, send, recv, device):
        return pltpu.make_async_remote_copy(
            src_ref=src, dst_ref=dst, send_sem=send, recv_sem=recv, device_id=device, device_id_type=MESH
        )

    def core_copy(chunk):
        return remote(
            feat.at[:, cols(chunk, (1 - core) * WIDTH)],
            frames.at[rows_at(2 + 4 * core, 256, 4), cols(chunk)],
            core_send.at[chunk],
            core_recv.at[chunk],
            place.other_core(),
        )

    def halo_copy(chunk, target):
        return remote(
            feat.at[512:1024, cols(chunk, target * WIDTH)],
            frames.at[0:512, cols(chunk)],
            halo_send.at[chunk, target],
            halo_recv.at[chunk],
            place.device(x + 1, y, z, target),
        )

    def low_copy(chunk):
        return remote(
            recon.at[384:576, cols(chunk)],
            recon.at[0:192, cols(chunk)],
            low_send.at[chunk],
            low_recv.at[chunk],
            place.device(x + 1, y, z, core),
        )

    def high_copy(chunk):
        return remote(
            recon.at[192:384, cols(chunk)],
            recon.at[576:768, cols(chunk)],
            high_send.at[chunk],
            high_recv.at[chunk],
            place.device(x - 1, y, z, core),
        )

    for chunk in range(NCH):
        own_copy(chunk).start()

    barrier = pltpu.get_barrier_semaphore()
    partners = [place.other_core()] + [place.along(axis, step) for axis in range(3) for step in (1, 2, 3)]
    partners += [place.device(lax.rem(x + step, 4), y, z, 1 - core) for step in (1, 3)]
    for device in partners:
        pl.semaphore_signal(barrier, inc=1, device_id=device, device_id_type=MESH)
    pl.semaphore_wait(barrier, len(partners))

    for chunk in range(NCH):
        core_copy(chunk).start()

    @pl.when((core == 1) & inner_high)
    def _():
        for chunk in range(NCH):
            for target in (0, 1):
                halo_copy(chunk, target).start()

    @pl.when(clip_start)
    def _():
        frames[0:512] = jnp.zeros((512, WIDTH), jnp.bfloat16)
        recon[0:192] = jnp.zeros((192, WIDTH), jnp.bfloat16)

    @pl.when(clip_end)
    def _():
        recon[576:768] = jnp.zeros((192, WIDTH), jnp.bfloat16)

    ends = []
    for span in range(4):
        ends.append(spans[0, span] + (ends[-1] if ends else 0))

    def span_of(frame):
        return sum((frame >= end).astype(jnp.int32) for end in ends)

    def tap_mask(local, tap):
        frame = 8 * x + local
        same = (span_of(frame) == span_of(frame - tap)) & (frame >= tap)
        return jnp.where(same, 1.0, 0.0).astype(F32)

    def valid(local):
        frame = 8 * x + local
        return jnp.where((frame >= 0) & (frame < 32), 1.0, 0.0).astype(F32)

    row, column = (lax.broadcasted_iota(jnp.int32, (256, 256), axis) for axis in (0, 1))
    same = jnp.where(row == column, 1.0, 0.0).astype(jnp.bfloat16)
    for tap in range(3):
        block = 256 * (2 - tap)
        conv_t[block : block + 256] = dot_nt(same, conv_w[tap]).astype(jnp.bfloat16)
        second_t[256 * tap : 256 * tap + 256] = dot_nt(same, second_w[tap]).astype(jnp.bfloat16)

    def mask_weights(local, carry):
        for block, tap in ((0, 2), (1, 1), (2, 0)):
            weight = conv_t[256 * block : 256 * block + 256].astype(F32) * tap_mask(local, tap)
            masked[rows_at(3 * local + block, 256)] = weight.astype(jnp.bfloat16)
        return carry

    lax.fori_loop(0, 8, mask_weights, 0)
    for acc in (acc_conv, acc_second, acc_first, acc_out, acc_head):
        acc[...] = jnp.zeros_like(acc)

    head = head_w[...].astype(F32)
    sign = (2 * labels[0] - 1).astype(F32)

    def positions(frame, chunk):
        return slice(frame * WIDTH + chunk * SC, frame * WIDTH + chunk * SC + SC)

    def turn(frame, chunk):
        turned[positions(frame, chunk)] = frames[rows_at(frame, 256), cols(chunk)].T

    def decode(local, chunk):
        window = jnp.concatenate([turned[positions(local + tap, chunk)] for tap in range(3)], axis=1)
        pre = dot(window, masked[rows_at(local, 768)])
        gate = 0.5 * jnp.tanh(0.5 * pre) + 0.5
        silu = pre * gate
        value = (turned[positions(local + 2, chunk)].astype(F32) + silu).astype(jnp.bfloat16)
        hidden[positions(local, chunk)] = value
        slopes[positions(local, chunk)] = gate + silu * (1.0 - gate)
        recon[rows_at(local + 4, 48), cols(chunk)] = dot_nt(ow[...], value).astype(jnp.bfloat16)

    def decode_inner(chunk):
        own_copy(chunk).wait()
        core_copy(chunk).wait_recv()
        for frame in range(2, 10):
            turn(frame, chunk)
            if frame >= 4:
                decode(frame - 2, chunk)

    def decode_halo(chunk):
        @pl.when(inner_low)
        def _():
            halo_copy(chunk, 0).wait_recv()

        for frame in (0, 1):
            turn(frame, chunk)
        for local in (0, 1):
            decode(local, chunk)

        @pl.when(inner_high)
        def _():
            low_copy(chunk).start()

        @pl.when(inner_low)
        def _():
            high_copy(chunk).start()

    def first_layer(local, where):
        pre = dot(recon[rows_at(local + 3, 48, 3), where].T, fwt[...])
        if 0 <= local < 8:
            value = jnp.maximum(pre, 0.2 * pre)
        else:
            on = valid(local)
            value = pre * jnp.where(pre > 0, on, 0.2 * on)
        value = value.astype(jnp.bfloat16)
        disc[rows_at(local + 3, SC)] = value
        if -1 <= local < 9:
            disc_t[rows_at(local + 1, 256)] = value.T

    def second_layer(local):
        window = jnp.concatenate([disc[rows_at(local + 2 + tap, SC)] for tap in range(3)], axis=1)
        pre = dot(window, second_t[...])
        act = jnp.maximum(pre, 0.2 * pre)
        logits = jnp.sum(act * head, axis=1, keepdims=True)
        scale = -sign * loss_scale * (1.0 if 0 <= local < 8 else valid(local))
        grad = scale / (1.0 + jnp.exp(sign * logits))
        if 0 <= local < 8:
            acc_head[...] += jnp.sum((act * grad).reshape(SC // 8, 8, 256), axis=0)
        second[rows_at(local + 2, SC)] = (jnp.where(pre > 0, head, 0.2 * head) * grad).astype(jnp.bfloat16)

    def first_back(local):
        window = jnp.concatenate([second[rows_at(local + 3 - tap, SC)] for tap in range(3)], axis=1)
        back = dot(window, second_w[...].reshape(768, 256))
        on = 1.0 if 0 <= local < 8 else valid(local)
        slope = jnp.where(disc[rows_at(local + 3, SC)].astype(F32) > 0, on, 0.2 * on)
        value = (back * slope).astype(jnp.bfloat16)
        first[rows_at(local + 1, SC)] = value
        parts[rows_at(local + 1, 144)] = dot_nt(fwt[...], value)

    def recon_back(local, where):
        total = (
            parts[pl.ds((local + 2) * 144, 48)]
            + parts[pl.ds((local + 1) * 144 + 48, 48)]
            + parts[pl.ds(local * 144 + 96, 48)]
        )
        rgrad[rows_at(local, 48), where] = total.astype(jnp.bfloat16)

    def wide(ref, step, height, where=slice(None)):
        return jnp.concatenate([ref[start : start + height, where] for start in step], axis=1)

    def weight_grads(chunk):
        own, where = range(8), cols(chunk)
        acc_second[...] += dot(wide(disc_t, [t * 256 for t in own], 768), second[2 * SC : 10 * SC])
        acc_first[...] += dot(wide(recon, [(t + 3) * 48 for t in own], 144, where), first[SC : 9 * SC])
        value = jnp.concatenate([hidden[positions(t, chunk)] for t in own], axis=0)
        acc_out[...] += dot(wide(rgrad, [t * 48 for t in own], 48, where), value)

    for chunk in range(NCH):
        decode_inner(chunk)
    decode_halo(0)

    for chunk in range(NCH):
        where = cols(chunk)

        @pl.when(inner_low)
        def _():
            low_copy(chunk).wait_recv()

        @pl.when(inner_high)
        def _():
            high_copy(chunk).wait_recv()

        for step in range(-3, 14):
            if step < 11:
                first_layer(step, where)
            if -2 <= step - 2 < 10:
                second_layer(step - 2)
            if -1 <= step - 4 < 9:
                first_back(step - 4)
            if 0 <= step - 6:
                recon_back(step - 6, where)

        if chunk + 1 < NCH:
            decode_halo(chunk + 1)
        weight_grads(chunk)

    for part in range(3):
        grads1[part, 0:256] = acc_second[256 * part : 256 * part + 256].T
        grads1[part, 256:304] = acc_first[48 * part : 48 * part + 48]
        grads1[part, 304:320] = acc_out[16 * part : 16 * part + 16]
        grads1[part, 320:384] = jnp.zeros((64, 256), F32)
    grads1[0, 320:328] = jnp.broadcast_to(jnp.sum(acc_head[...], axis=0, keepdims=True), (8, 256))

    reduce1 = Reducer(place, grads1, total1, bufs[:6], send1, recv1)
    reduce2 = Reducer(place, grads2, total2, bufs[6:], send2, recv2)
    steps1, steps2 = reduce1.steps(), reduce2.steps()

    def conv_back(local):
        back = dot(rgrad[rows_at(local, 48)].T, ow[...])
        delta = (back * slopes[rows_at(local, WIDTH)]).astype(jnp.bfloat16)
        result = dot(frames[rows_at(local, 256, 3)], delta)
        for block, tap in ((0, 2), (1, 1), (2, 0)):
            rows = slice(256 * block, 256 * block + 256)
            acc_conv[rows] += result[rows] * tap_mask(local, tap)

    steps1[0]()
    for pair in range(4):
        conv_back(2 * pair)
        conv_back(2 * pair + 1)
        if pair < 3:
            steps1[pair + 1]()
    for tap in range(3):
        grads2[tap] = acc_conv[256 * (2 - tap) : 256 * (2 - tap) + 256].T
    steps2[0]()
    for index in range(4, 8):
        steps1[index]()
        steps2[index - 3]()
    for index in range(5, 8):
        steps2[index]()

    reduce1.finish()
    reduce2.finish()
    for chunk in range(NCH):
        core_copy(chunk).wait_send()

        @pl.when((core == 1) & inner_high)
        def _():
            halo_copy(chunk, 0).wait_send()
            halo_copy(chunk, 1).wait_send()

        @pl.when(inner_high)
        def _():
            low_copy(chunk).wait_send()

        @pl.when(inner_low)
        def _():
            high_copy(chunk).wait_send()


def per_device(
    features, conv_weight, out_weight, first_weight, second_weight, head_weight, span_lengths, labels
):
    clips, frame_count, channels, positions = features.shape
    total_count = (
        clips * lax.axis_size("dp") * lax.axis_size("group") * frame_count * lax.axis_size("tm") * positions
    )
    loss_scale = float(total_count) ** (-0.5)
    bf16 = jnp.bfloat16
    operands = (
        span_lengths,
        labels,
        features.reshape(frame_count * channels, positions),
        conv_weight,
        out_weight,
        jnp.swapaxes(first_weight, 1, 2).reshape(144, 256),
        second_weight,
        head_weight.reshape(1, 256),
    )
    smem, vmem = pl.BlockSpec(memory_space=pltpu.SMEM), pl.BlockSpec(memory_space=pltpu.VMEM)
    dma = pltpu.SemaphoreType.DMA
    totals = pl.pallas_call(
        functools.partial(block_kernel, loss_scale),
        out_shape=(
            jax.ShapeDtypeStruct((3, 384, 256), F32),
            jax.ShapeDtypeStruct((3, 256, 256), bf16),
        ),
        in_specs=[smem, smem, pl.BlockSpec(memory_space=pl.ANY)] + [vmem] * 5,
        out_specs=(vmem, vmem),
        scratch_shapes=[
            pltpu.VMEM((2560, WIDTH), bf16),
            pltpu.VMEM((10 * WIDTH, 256), bf16),
            pltpu.VMEM((8 * WIDTH, 256), bf16),
            pltpu.VMEM((8 * WIDTH, 256), F32),
            pltpu.VMEM((768, WIDTH), bf16),
            pltpu.VMEM((14 * SC, 256), bf16),
            pltpu.VMEM((10 * 256, SC), bf16),
            pltpu.VMEM((12 * SC, 256), bf16),
            pltpu.VMEM((10 * SC, 256), bf16),
            pltpu.VMEM((10 * 144, SC), F32),
            pltpu.VMEM((8 * 48, WIDTH), bf16),
            pltpu.VMEM((768, 256), bf16),
            pltpu.VMEM((8 * 768, 256), bf16),
            pltpu.VMEM((768, 256), bf16),
            pltpu.VMEM((768, 256), F32),
            pltpu.VMEM((768, 256), F32),
            pltpu.VMEM((144, 256), F32),
            pltpu.VMEM((48, 256), F32),
            pltpu.VMEM((8, 256), F32),
            pltpu.VMEM((3, 384, 256), F32),
            pltpu.VMEM((3, 256, 256), F32),
            dma((NCH,)),
            dma((NCH,)),
            dma((NCH,)),
            dma((NCH, 2)),
            dma((NCH,)),
            dma((NCH,)),
            dma((NCH,)),
            dma((NCH,)),
            dma((NCH,)),
            dma((N_SLOTS,)),
            dma((N_SLOTS,)),
            dma((N_SLOTS,)),
            dma((N_SLOTS,)),
        ]
        + reduce_scratch(384)
        + reduce_scratch(256),
        compiler_params=pltpu.CompilerParams(
            collective_id=0, has_side_effects=True, vmem_limit_bytes=58 * MIB
        ),
    )(*operands)
    conv, out, first, second, head = pl.pallas_call(
        finish_kernel,
        out_shape=(
            jax.ShapeDtypeStruct((3, 256, 256), F32),
            jax.ShapeDtypeStruct((48, 256), F32),
            jax.ShapeDtypeStruct((3, 48, 256), F32),
            jax.ShapeDtypeStruct((3, 256, 256), F32),
            jax.ShapeDtypeStruct((1, 256), F32),
        ),
        in_specs=[vmem, vmem],
        out_specs=(vmem,) * 5,
        compiler_params=pltpu.CompilerParams(vmem_limit_bytes=16 * MIB),
    )(*totals)
    return conv, out, jnp.swapaxes(first, 1, 2), second, head.reshape(256)


def solution(mesh):
    placed = (
        P(("dp", "group"), "tm", None, None),
        P(),
        P(),
        P(),
        P(),
        P(),
        P(("dp", "group"), None),
        P(("dp", "group")),
    )
    return jax.shard_map(
        per_device, mesh=mesh, in_specs=placed, out_specs=(P(), P(), P(), P(), P()), check_vma=False
    )
```

```python
import functools

import jax
import jax.numpy as jnp
from jax import lax
from jax.experimental import pallas as pl
from jax.experimental.pallas import tpu as pltpu
from jax.sharding import PartitionSpec as P

MESH = pl.DeviceIdType.MESH
F32 = jnp.float32


class Place:
    def __init__(self):
        tm, dp, group = (lax.axis_index(name) for name in ("tm", "dp", "group"))
        self.core = lax.rem(tm, 2)
        self.at = (tm // 2, dp // 2, 2 * group + lax.rem(dp, 2))

    def device(self, x, y, z, core):
        return (2 * x + core, 2 * y + lax.rem(z, 2), z // 2)

    def along(self, axis, step):
        place = list(self.at)
        place[axis] = lax.rem(place[axis] + step, 4)
        return self.device(*place, self.core)

    def other_core(self):
        return self.device(*self.at, 1 - self.core)


class Reducer:
    def __init__(self, place, grads, total, bufs, send_sems, recv_sems):
        self.place, self.grads, self.total = (place, grads, total)
        self.sum1, self.in1, self.sum2, self.in2, self.in3 = bufs
        self.send_sems, self.recv_sems = (send_sems, recv_sems)
        self.rows = grads.shape[1]
        self.sent = []
        self.axes = [tuple((part + i) % 3 for i in range(3)) for part in range(3)]

    def copy(self, src, dst, slot, device):
        return pltpu.make_async_remote_copy(
            src_ref=src,
            dst_ref=dst,
            send_sem=self.send_sems.at[slot],
            recv_sem=self.recv_sems.at[slot],
            device_id=device,
            device_id_type=MESH,
        )

    def start(self, *args):
        copy = self.copy(*args)
        copy.start()
        self.sent.append(copy)

    def lanes(self, core):
        return pl.ds(pl.multiple_of(core * 128, 128), 128)

    def block(self, index, size):
        return pl.ds(pl.multiple_of(index * size, size), size)

    def slot(self, stage, part, step):
        return 3 + (stage * 3 + part) * 3 + step - 1

    def core_send(self, part):
        place = self.place
        src = self.grads.at[part, :, self.lanes(1 - place.core)]
        self.start(src, self.sum1.at[part], part, place.other_core())

    def core_sum(self, part):
        place = self.place
        self.copy(self.sum1.at[part], self.sum1.at[part], part, place.other_core()).wait_recv()
        self.sum1[part] = self.grads[part, :, self.lanes(place.core)] + self.sum1[part]

    def scatter_send(self, part, level):
        axis = self.axes[part][level]
        source, landing = ((self.sum1, self.in1), (self.sum2, self.in2))[level]
        size = landing.shape[2]
        for step in (1, 2, 3):
            target = lax.rem(self.place.at[axis] + step, 4)
            self.start(
                source.at[part, self.block(target, size)],
                landing.at[part, step - 1],
                self.slot(level, part, step),
                self.place.along(axis, step),
            )

    def scatter_sum(self, part, level):
        axis = self.axes[part][level]
        source, landing = ((self.sum1, self.in1), (self.sum2, self.in2))[level]
        size = landing.shape[2]
        for step in (1, 2, 3):
            here = landing.at[part, step - 1]
            self.copy(here, here, self.slot(level, part, step), self.place.along(axis, step)).wait_recv()
        result = source[part, self.block(self.place.at[axis], size)]
        for step in (1, 2, 3):
            result = result + landing[part, step - 1]
        if level == 0:
            self.sum2[part] = result
        else:
            self.in3[part, self.place.at[self.axes[part][2]]] = result

    def swap_send(self, part):
        axis = self.axes[part][2]
        here = self.in3.at[part, self.place.at[axis]]
        for step in (1, 2, 3):
            self.start(here, here, self.slot(2, part, step), self.place.along(axis, step))

    def rows_of(self, part, level):
        first = self.place.at[self.axes[part][0]]
        if level == 0:
            return self.block(first, self.rows // 4)
        return self.block(4 * first + self.place.at[self.axes[part][1]], self.rows // 16)

    def swap_sum(self, part):
        axis = self.axes[part][2]
        for step in (1, 2, 3):
            here = self.in3.at[part, step]
            self.copy(here, here, self.slot(2, part, step), self.place.along(axis, step)).wait_recv()
        result = (self.in3[part, 0] + self.in3[part, 1]) + (self.in3[part, 2] + self.in3[part, 3])
        self.total[part, self.rows_of(part, 1), self.lanes(self.place.core)] = result.astype(self.total.dtype)

    def gather_send(self, part, level):
        axis = self.axes[part][level]
        here = self.total.at[part, self.rows_of(part, level), self.lanes(self.place.core)]
        for step in (1, 2, 3):
            self.start(here, here, self.slot(4 - level, part, step), self.place.along(axis, step))

    def gather_wait(self, part, level):
        axis = self.axes[part][level]
        here = self.total.at[part, self.rows_of(part, level), self.lanes(self.place.core)]
        for step in (1, 2, 3):
            self.copy(here, here, self.slot(4 - level, part, step), self.place.along(axis, step)).wait_recv()

    def back_send(self, part):
        here = self.total.at[part, :, self.lanes(self.place.core)]
        self.start(here, here, 48 + part, self.place.other_core())

    def back_wait(self, part):
        here = self.total.at[part, :, self.lanes(1 - self.place.core)]
        self.copy(here, here, 48 + part, self.place.other_core()).wait_recv()

    def steps(self):
        def each(*calls):
            def run():
                for part in range(3):
                    for call, *level in calls:
                        call(part, *level)

            return run

        return [
            each((self.core_send,)),
            each((self.core_sum,), (self.scatter_send, 0)),
            each((self.scatter_sum, 0), (self.scatter_send, 1)),
            each((self.scatter_sum, 1), (self.swap_send,)),
            each((self.swap_sum,), (self.gather_send, 1)),
            each((self.gather_wait, 1), (self.gather_send, 0)),
            each((self.gather_wait, 0), (self.back_send,)),
            each((self.back_wait,)),
        ]

    def finish(self):
        for copy in self.sent:
            copy.wait_send()


N_SLOTS = 51


def reduce_scratch(rows):
    return [
        pltpu.VMEM((3, rows, 128), F32),
        pltpu.VMEM((3, 3, rows // 4, 128), F32),
        pltpu.VMEM((3, rows // 4, 128), F32),
        pltpu.VMEM((3, 3, rows // 16, 128), F32),
        pltpu.VMEM((3, 4, rows // 16, 128), F32),
    ]


SC = 512
WIDTH = 1024
NCH = WIDTH // SC
MIB = 1024 * 1024


def dot(a, b):
    return jnp.dot(a, b, preferred_element_type=F32)


def dot_nt(a, b):
    return lax.dot_general(a, b, (((1,), (1,)), ((), ())), preferred_element_type=F32)


def rows_at(frame, height, count=1):
    start = frame * height
    return pl.ds(start if isinstance(start, int) else pl.multiple_of(start, height), height * count)


def finish_kernel(total1, total2, conv_out, out_out, first_out, second_out, head_out):
    for part in range(3):
        conv_out[part] = total2[part].astype(F32)
        second_out[part] = total1[part, 0:256]
        first_out[part] = total1[part, 256:304]
        out_out[16 * part : 16 * part + 16] = total1[part, 304:320]
    head_out[...] = total1[0, 320:321]


def block_kernel(
    loss_scale,
    spans, labels, feat, conv_w, ow, fwt, second_w, head_w,
    total1, total2,
    frames, turned, hidden, slopes, recon, disc, disc_t, second, first, parts, rgrad, conv_t, second_t,
    acc_conv, acc_second, acc_first, acc_out, acc_head, grads1, grads2,
    own_sem, core_send, core_recv, after_send, after_recv, before_send, before_recv,
    low_send, low_recv, high_send, high_recv,
    send1, recv1, send2, recv2, *bufs,
):
    place = Place()
    x, y, z = place.at
    core = place.core
    clip_start, clip_end = x == 0, x == 3
    inner_low, inner_high = x > 0, x < 3

    def cols(chunk, base=0):
        return pl.ds(pl.multiple_of(base + chunk * SC, SC), SC)

    def own_copy(chunk):
        return pltpu.make_async_copy(
            feat.at[:, cols(chunk, core * WIDTH)],
            frames.at[chunk, rows_at(1 + 4 * core, 256, 4)],
            own_sem.at[chunk],
        )

    def remote(src, dst, send, recv, device):
        return pltpu.make_async_remote_copy(
            src_ref=src, dst_ref=dst, send_sem=send, recv_sem=recv, device_id=device, device_id_type=MESH
        )

    def core_copy(chunk):
        return remote(
            feat.at[:, cols(chunk, (1 - core) * WIDTH)],
            frames.at[chunk, rows_at(1 + 4 * core, 256, 4)],
            core_send.at[chunk],
            core_recv.at[chunk],
            place.other_core(),
        )

    def after_copy(chunk):
        return remote(
            frames.at[chunk, 2048:2304],
            frames.at[chunk, 0:256],
            after_send.at[chunk],
            after_recv.at[chunk],
            place.device(x + 1, y, z, core),
        )

    def before_copy(chunk):
        return remote(
            frames.at[chunk, 256:512],
            frames.at[chunk, 2304:2560],
            before_send.at[chunk],
            before_recv.at[chunk],
            place.device(x - 1, y, z, core),
        )

    def low_copy(chunk):
        return remote(
            recon.at[chunk, 384:576],
            recon.at[chunk, 0:192],
            low_send.at[chunk],
            low_recv.at[chunk],
            place.device(x + 1, y, z, core),
        )

    def high_copy(chunk):
        return remote(
            recon.at[chunk, 192:384],
            recon.at[chunk, 576:768],
            high_send.at[chunk],
            high_recv.at[chunk],
            place.device(x - 1, y, z, core),
        )

    def to_both_sides(up, down, act):
        @pl.when(inner_high)
        def _():
            act(up)

        @pl.when(inner_low)
        def _():
            act(down)

    def send_halo(chunk):
        to_both_sides(after_copy(chunk), before_copy(chunk), lambda copy: copy.start())

    def await_halo(chunk):
        to_both_sides(before_copy(chunk), after_copy(chunk), lambda copy: copy.wait_recv())

    def send_recon(chunk):
        to_both_sides(low_copy(chunk), high_copy(chunk), lambda copy: copy.start())

    def await_recon(chunk):
        to_both_sides(high_copy(chunk), low_copy(chunk), lambda copy: copy.wait_recv())

    for chunk in range(NCH):
        own_copy(chunk).start()

    barrier = pltpu.get_barrier_semaphore()
    partners = [place.other_core()] + [place.along(axis, step) for axis in range(3) for step in (1, 2, 3)]
    for device in partners:
        pl.semaphore_signal(barrier, inc=1, device_id=device, device_id_type=MESH)
    pl.semaphore_wait(barrier, len(partners))

    for chunk in range(NCH):
        core_copy(chunk).start()

    @pl.when(clip_start)
    def _():
        for chunk in range(NCH):
            frames[chunk, 0:256] = jnp.zeros((256, SC), jnp.bfloat16)
            recon[chunk, 0:192] = jnp.zeros((192, SC), jnp.bfloat16)

    @pl.when(clip_end)
    def _():
        for chunk in range(NCH):
            frames[chunk, 2304:2560] = jnp.zeros((256, SC), jnp.bfloat16)
            recon[chunk, 576:768] = jnp.zeros((192, SC), jnp.bfloat16)

    ends = []
    for span in range(4):
        ends.append(spans[0, span] + (ends[-1] if ends else 0))

    def span_of(frame):
        return sum((frame >= end).astype(jnp.int32) for end in ends)

    def tap_mask(local, tap):
        frame = 8 * x + 1 + local
        same = (span_of(frame) == span_of(frame - tap)) & (frame >= tap) & (frame < 32)
        return jnp.where(same, 1.0, 0.0).astype(F32)

    def valid(local):
        frame = 8 * x + 1 + local
        return jnp.where((frame >= 0) & (frame < 32), 1.0, 0.0).astype(F32)

    row, column = (lax.broadcasted_iota(jnp.int32, (256, 256), axis) for axis in (0, 1))
    same = jnp.where(row == column, 1.0, 0.0).astype(jnp.bfloat16)
    for tap in range(3):
        block = 256 * (2 - tap)
        conv_t[block : block + 256] = dot_nt(same, conv_w[tap]).astype(jnp.bfloat16)
        second_t[256 * tap : 256 * tap + 256] = dot_nt(same, second_w[tap]).astype(jnp.bfloat16)

    for acc in (acc_conv, acc_second, acc_first, acc_out, acc_head):
        acc[...] = jnp.zeros_like(acc)

    head = head_w[...].astype(F32)
    sign = (2 * labels[0] - 1).astype(F32)

    def positions(frame, chunk):
        return slice(frame * WIDTH + chunk * SC, frame * WIDTH + chunk * SC + SC)

    def turn(frame, chunk):
        turned[positions(frame, chunk)] = frames[chunk, rows_at(frame, 256)].T

    def activate(pre, center, slot, recon_slot, chunk):
        gate = 0.5 * jnp.tanh(0.5 * pre) + 0.5
        silu = pre * gate
        value = (turned[positions(center, chunk)].astype(F32) + silu).astype(jnp.bfloat16)
        hidden[positions(slot, chunk)] = value
        slopes[positions(slot, chunk)] = gate + silu * (1.0 - gate)
        recon[chunk, rows_at(recon_slot, 48)] = dot_nt(ow[...], value).astype(jnp.bfloat16)

    def decode(local, chunk):
        window = jnp.concatenate([turned[positions(local + tap, chunk)] for tap in range(3)], axis=1)
        weight = [
            conv_t[256 * block : 256 * block + 256]
            * jnp.full((1, 256), tap_mask(local, 2 - block), F32).astype(jnp.bfloat16)
            for block in range(3)
        ]
        pre = dot(window, jnp.concatenate(weight, axis=0))
        activate(pre, local + 2, local, local + 4, chunk)

    def await_frames(chunk):
        own_copy(chunk).wait()
        core_copy(chunk).wait_recv()

    def decode_inner(chunk):
        for frame in range(1, 9):
            turn(frame, chunk)
            if frame >= 3:
                decode(frame - 2, chunk)

        @pl.when(clip_start)
        def _():
            activate(dot(turned[positions(1, chunk)], conv_t[512:768]), 1, 8, 3, chunk)

    def decode_halo(chunk):
        await_halo(chunk)
        for frame in (0, 9):
            turn(frame, chunk)
        for local in (0, 7):
            decode(local, chunk)
        send_recon(chunk)

    def first_layer(local, chunk):
        pre = dot(recon[chunk, rows_at(local + 3, 48, 3)].T, fwt[...])
        if 0 <= local < 7:
            value = jnp.maximum(pre, 0.2 * pre)
        else:
            on = valid(local)
            value = pre * jnp.where(pre > 0, on, 0.2 * on)
        value = value.astype(jnp.bfloat16)
        disc[rows_at(local + 3, SC)] = value
        if -1 <= local < 9:
            disc_t[rows_at(local + 1, 256)] = value.T

    def second_layer(local):
        window = jnp.concatenate([disc[rows_at(local + 2 + tap, SC)] for tap in range(3)], axis=1)
        pre = dot(window, second_t[...])
        act = jnp.maximum(pre, 0.2 * pre)
        logits = jnp.sum(act * head, axis=1, keepdims=True)
        scale = -sign * loss_scale * (1.0 if 0 <= local < 7 else valid(local))
        grad = scale / (1.0 + jnp.exp(sign * logits))
        if -1 <= local < 8:
            share = grad * jnp.where(clip_start, 1.0, 0.0).astype(F32) if local < 0 else grad
            acc_head[...] += jnp.sum((act * share).reshape(SC // 8, 8, 256), axis=0)
        second[rows_at(local + 2, SC)] = (jnp.where(pre > 0, head, 0.2 * head) * grad).astype(jnp.bfloat16)

    def first_back(local):
        window = jnp.concatenate([second[rows_at(local + 3 - tap, SC)] for tap in range(3)], axis=1)
        back = dot(window, second_w[...].reshape(768, 256))
        on = 1.0 if 0 <= local < 7 else valid(local)
        slope = jnp.where(disc[rows_at(local + 3, SC)].astype(F32) > 0, on, 0.2 * on)
        value = (back * slope).astype(jnp.bfloat16)
        first[rows_at(local + 1, SC)] = value
        parts[rows_at(local + 1, 144)] = dot_nt(fwt[...], value)

    def recon_back(local, where):
        total = (
            parts[pl.ds((local + 2) * 144, 48)]
            + parts[pl.ds((local + 1) * 144 + 48, 48)]
            + parts[pl.ds(local * 144 + 96, 48)]
        )
        rgrad[rows_at(local, 48), where] = total.astype(jnp.bfloat16)

    def recon_back_first(where):
        rgrad[rows_at(8, 48), where] = (parts[144:192] + parts[48:96]).astype(jnp.bfloat16)

    def wide(blocks):
        return jnp.concatenate(blocks, axis=1)

    def weight_grads(chunk):
        own, where = range(8), cols(chunk)
        left = wide([disc_t[t * 256 : t * 256 + 768] for t in own])
        acc_second[...] += dot(left, second[2 * SC : 10 * SC])
        left = wide([recon[chunk, (t + 3) * 48 : (t + 6) * 48] for t in own])
        acc_first[...] += dot(left, first[SC : 9 * SC])
        value = jnp.concatenate([hidden[positions(t, chunk)] for t in own], axis=0)
        acc_out[...] += dot(wide([rgrad[t * 48 : t * 48 + 48, where] for t in own]), value)

        @pl.when(clip_start)
        def _():
            acc_second[256:768] += dot(disc_t[0:512], second[SC : 2 * SC])
            acc_first[48:144] += dot(recon[chunk, 144:240], first[0:SC])
            acc_out[...] += dot(rgrad[384:432, where], hidden[positions(8, chunk)])

    await_frames(0)
    send_halo(0)
    decode_inner(0)
    decode_halo(0)
    for chunk in range(1, NCH):
        await_frames(chunk)
        decode_inner(chunk)

    for chunk in range(NCH):
        where = cols(chunk)
        await_recon(chunk)
        if chunk + 1 < NCH:
            send_halo(chunk + 1)
        for step in range(-3, 14):
            if step < 11:
                first_layer(step, chunk)
            if -2 <= step - 2 < 10:
                second_layer(step - 2)
            if -1 <= step - 4 < 9:
                first_back(step - 4)
            if 0 <= step - 6:
                recon_back(step - 6, where)
        recon_back_first(where)
        if chunk + 1 < NCH:
            decode_halo(chunk + 1)
        weight_grads(chunk)

    for part in range(3):
        grads1[part, 0:256] = acc_second[256 * part : 256 * part + 256].T
        grads1[part, 256:304] = acc_first[48 * part : 48 * part + 48]
        grads1[part, 304:320] = acc_out[16 * part : 16 * part + 16]
        grads1[part, 320:384] = jnp.zeros((64, 256), F32)
    grads1[0, 320:328] = jnp.broadcast_to(jnp.sum(acc_head[...], axis=0, keepdims=True), (8, 256))

    reduce1 = Reducer(place, grads1, total1, bufs[:5], send1, recv1)
    reduce2 = Reducer(place, grads2, total2, bufs[5:], send2, recv2)
    steps1, steps2 = reduce1.steps(), reduce2.steps()

    def conv_back(local):
        back = dot(rgrad[rows_at(local, 48)].T, ow[...])
        delta = (back * slopes[rows_at(local, WIDTH)]).astype(jnp.bfloat16)
        result = dot(wide([frames[chunk, rows_at(local, 256, 3)] for chunk in range(NCH)]), delta)
        for block, tap in ((0, 2), (1, 1), (2, 0)):
            rows = slice(256 * block, 256 * block + 256)
            acc_conv[rows] += result[rows] * tap_mask(local, tap)

    def conv_back_first():
        back = dot(rgrad[rows_at(8, 48)].T, ow[...])
        delta = (back * slopes[rows_at(8, WIDTH)]).astype(jnp.bfloat16)
        acc_conv[512:768] += dot(wide([frames[chunk, 256:512] for chunk in range(NCH)]), delta)

    steps1[0]()
    pl.when(clip_start)(conv_back_first)
    for pair in range(4):
        conv_back(2 * pair)
        conv_back(2 * pair + 1)
        if pair < 3:
            steps1[pair + 1]()
    for tap in range(3):
        grads2[tap] = acc_conv[256 * (2 - tap) : 256 * (2 - tap) + 256].T
    steps2[0]()
    for index in range(4, 8):
        steps1[index]()
        steps2[index - 3]()
    for index in range(5, 8):
        steps2[index]()

    reduce1.finish()
    reduce2.finish()
    for chunk in range(NCH):
        core_copy(chunk).wait_send()

        to_both_sides(after_copy(chunk), before_copy(chunk), lambda copy: copy.wait_send())
        to_both_sides(low_copy(chunk), high_copy(chunk), lambda copy: copy.wait_send())


def per_device(
    features, conv_weight, out_weight, first_weight, second_weight, head_weight, span_lengths, labels
):
    clips, frame_count, channels, positions = features.shape
    total_count = (
        clips * lax.axis_size("dp") * lax.axis_size("group") * frame_count * lax.axis_size("tm") * positions
    )
    loss_scale = float(total_count) ** (-0.5)
    bf16 = jnp.bfloat16
    operands = (
        span_lengths,
        labels,
        features.reshape(frame_count * channels, positions),
        conv_weight,
        out_weight,
        jnp.swapaxes(first_weight, 1, 2).reshape(144, 256),
        second_weight,
        head_weight.reshape(1, 256),
    )
    smem, vmem = pl.BlockSpec(memory_space=pltpu.SMEM), pl.BlockSpec(memory_space=pltpu.VMEM)
    dma = pltpu.SemaphoreType.DMA
    totals = pl.pallas_call(
        functools.partial(block_kernel, loss_scale),
        out_shape=(
            jax.ShapeDtypeStruct((3, 384, 256), F32),
            jax.ShapeDtypeStruct((3, 256, 256), bf16),
        ),
        in_specs=[smem, smem, pl.BlockSpec(memory_space=pl.ANY)] + [vmem] * 5,
        out_specs=(vmem, vmem),
        scratch_shapes=[
            pltpu.VMEM((NCH, 2560, SC), bf16),
            pltpu.VMEM((10 * WIDTH, 256), bf16),
            pltpu.VMEM((9 * WIDTH, 256), bf16),
            pltpu.VMEM((9 * WIDTH, 256), F32),
            pltpu.VMEM((NCH, 768, SC), bf16),
            pltpu.VMEM((14 * SC, 256), bf16),
            pltpu.VMEM((10 * 256, SC), bf16),
            pltpu.VMEM((12 * SC, 256), bf16),
            pltpu.VMEM((10 * SC, 256), bf16),
            pltpu.VMEM((10 * 144, SC), F32),
            pltpu.VMEM((9 * 48, WIDTH), bf16),
            pltpu.VMEM((768, 256), bf16),
            pltpu.VMEM((768, 256), bf16),
            pltpu.VMEM((768, 256), F32),
            pltpu.VMEM((768, 256), F32),
            pltpu.VMEM((144, 256), F32),
            pltpu.VMEM((48, 256), F32),
            pltpu.VMEM((8, 256), F32),
            pltpu.VMEM((3, 384, 256), F32),
            pltpu.VMEM((3, 256, 256), F32),
            dma((NCH,)),
            dma((NCH,)),
            dma((NCH,)),
            dma((NCH,)),
            dma((NCH,)),
            dma((NCH,)),
            dma((NCH,)),
            dma((NCH,)),
            dma((NCH,)),
            dma((NCH,)),
            dma((NCH,)),
            dma((N_SLOTS,)),
            dma((N_SLOTS,)),
            dma((N_SLOTS,)),
            dma((N_SLOTS,)),
        ]
        + reduce_scratch(384)
        + reduce_scratch(256),
        compiler_params=pltpu.CompilerParams(
            collective_id=0, has_side_effects=True, vmem_limit_bytes=58 * MIB
        ),
    )(*operands)
    conv, out, first, second, head = pl.pallas_call(
        finish_kernel,
        out_shape=(
            jax.ShapeDtypeStruct((3, 256, 256), F32),
            jax.ShapeDtypeStruct((48, 256), F32),
            jax.ShapeDtypeStruct((3, 48, 256), F32),
            jax.ShapeDtypeStruct((3, 256, 256), F32),
            jax.ShapeDtypeStruct((1, 256), F32),
        ),
        in_specs=[vmem, vmem],
        out_specs=(vmem,) * 5,
        compiler_params=pltpu.CompilerParams(vmem_limit_bytes=16 * MIB),
    )(*totals)
    return conv, out, jnp.swapaxes(first, 1, 2), second, head.reshape(256)


def solution(mesh):
    placed = (
        P(("dp", "group"), "tm", None, None),
        P(),
        P(),
        P(),
        P(),
        P(),
        P(("dp", "group"), None),
        P(("dp", "group")),
    )
    return jax.shard_map(
        per_device, mesh=mesh, in_specs=placed, out_specs=(P(), P(), P(), P(), P()), check_vma=False
    )
```

```python
import functools

import jax
import jax.numpy as jnp
from jax import lax
from jax.experimental import pallas as pl
from jax.experimental.pallas import tpu as pltpu
from jax.sharding import PartitionSpec as P

MESH = pl.DeviceIdType.MESH
F32 = jnp.float32


class Place:
    def __init__(self):
        tm, dp, group = (lax.axis_index(name) for name in ("tm", "dp", "group"))
        self.core = lax.rem(tm, 2)
        self.at = (tm // 2, dp // 2, 2 * group + lax.rem(dp, 2))

    def device(self, x, y, z, core):
        return (2 * x + core, 2 * y + lax.rem(z, 2), z // 2)

    def along(self, axis, step, core=None):
        place = list(self.at)
        place[axis] = lax.rem(place[axis] + step, 4)
        return self.device(*place, self.core if core is None else core)

    def other_core(self):
        return self.device(*self.at, 1 - self.core)


class Reducer:
    def __init__(self, place, grads, total, bufs, send_sems, recv_sems):
        self.place, self.grads, self.total = (place, grads, total)
        self.in1, self.in2, self.in3 = bufs
        self.send_sems, self.recv_sems = (send_sems, recv_sems)
        self.size = grads.shape[1] // 8
        self.sent = []

    def axis(self, part, level):
        return (part + level) % 3

    def copy(self, src, dst, slot, device):
        return pltpu.make_async_remote_copy(
            src_ref=src,
            dst_ref=dst,
            send_sem=self.send_sems.at[slot],
            recv_sem=self.recv_sems.at[slot],
            device_id=device,
            device_id_type=MESH,
        )

    def start(self, *args):
        copy = self.copy(*args)
        copy.start()
        self.sent.append(copy)

    def await_copy(self, ref, slot):
        self.copy(ref, ref, slot, self.place.other_core()).wait_recv()

    def index(self, part):
        return 2 * self.place.at[self.axis(part, 0)] + self.place.core

    def block(self, index):
        return pl.ds(pl.multiple_of(index * self.size, self.size), self.size)

    def member(self, part, index):
        place = list(self.place.at)
        place[self.axis(part, 0)] = index // 2
        return self.place.device(*place, lax.rem(index, 2))

    def scatter_send(self, part):
        for step in range(1, 8):
            target = lax.rem(self.index(part) + step, 8)
            src = self.grads.at[part, self.block(target)]
            self.start(src, self.in1.at[part, step - 1], 20 * part + step - 1, self.member(part, target))

    def scatter_sum(self, part):
        for step in range(1, 8):
            self.await_copy(self.in1.at[part, step - 1], 20 * part + step - 1)
        result = self.grads[part, self.block(self.index(part))]
        for step in range(1, 8):
            result = result + self.in1[part, step - 1]
        self.in2[part, self.place.at[self.axis(part, 1)]] = result

    def swap_send(self, part, level):
        axis = self.axis(part, level)
        here = (self.in2, self.in3)[level - 1].at[part, self.place.at[axis]]
        for step in (1, 2, 3):
            self.start(here, here, 20 * part + 3 + 3 * level + step, self.place.along(axis, step))

    def swap_sum(self, part, level):
        held = (self.in2, self.in3)[level - 1]
        for step in (1, 2, 3):
            self.await_copy(held.at[part, step], 20 * part + 3 + 3 * level + step)
        result = (held[part, 0] + held[part, 1]) + (held[part, 2] + held[part, 3])
        if level == 1:
            self.in3[part, self.place.at[self.axis(part, 2)]] = result
        else:
            self.total[part, self.block(self.index(part))] = result.astype(self.total.dtype)

    def gather_send(self, part):
        here = self.total.at[part, self.block(self.index(part))]
        for step in range(1, 8):
            target = lax.rem(self.index(part) + step, 8)
            self.start(here, here, 20 * part + 12 + step, self.member(part, target))

    def gather_wait(self, part):
        here = self.total.at[part, self.block(self.index(part))]
        for step in range(1, 8):
            self.await_copy(here, 20 * part + 12 + step)

    def steps(self):
        def each(*calls):
            def run():
                for part in range(3):
                    for call, *level in calls:
                        call(part, *level)

            return run

        return [
            each((self.scatter_send,)),
            each((self.scatter_sum,), (self.swap_send, 1)),
            each((self.swap_sum, 1), (self.swap_send, 2)),
            each((self.swap_sum, 2), (self.gather_send,)),
            each((self.gather_wait,)),
        ]

    def finish(self):
        for copy in self.sent:
            copy.wait_send()


N_SLOTS = 60


def reduce_scratch(rows):
    size = rows // 8
    return [
        pltpu.VMEM((3, 7, size, 256), F32),
        pltpu.VMEM((3, 4, size, 256), F32),
        pltpu.VMEM((3, 4, size, 256), F32),
    ]


SC = 512
WIDTH = 1024
NCH = WIDTH // SC
MIB = 1024 * 1024


def dot(a, b):
    return jnp.dot(a, b, preferred_element_type=F32)


def dot_nt(a, b):
    return lax.dot_general(a, b, (((1,), (1,)), ((), ())), preferred_element_type=F32)


def rows_at(frame, height, count=1):
    start = frame * height
    return pl.ds(start if isinstance(start, int) else pl.multiple_of(start, height), height * count)


def finish_kernel(total1, total2, conv_out, out_out, first_out, second_out, head_out):
    for part in range(3):
        conv_out[part] = total2[part].astype(F32)
        second_out[part] = total1[part, 0:256].astype(F32)
        first_out[part] = total1[part, 256:304].astype(F32)
        out_out[16 * part : 16 * part + 16] = total1[part, 304:320].astype(F32)
    head_out[...] = total1[0, 320:336].astype(F32)[0:1]


def block_kernel(
    loss_scale,
    spans, labels, feat, conv_w, ow, fwt, second_w, head_w,
    total1, total2,
    frames, turned, hidden, slopes, recon, disc, disc_t, second, first, parts, rgrad, conv_t, second_t,
    acc_second, acc_first, acc_out, acc_head, grads1, grads2,
    own_sem, core_send, core_recv, after_send, after_recv, before_send, before_recv,
    low_send, low_recv, high_send, high_recv,
    send1, recv1, send2, recv2, *bufs,
):
    place = Place()
    x, y, z = place.at
    core = place.core
    clip_start, clip_end = x == 0, x == 3
    inner_low, inner_high = x > 0, x < 3

    def cols(chunk, base=0):
        return pl.ds(pl.multiple_of(base + chunk * SC, SC), SC)

    def own_copy(chunk):
        return pltpu.make_async_copy(
            feat.at[:, cols(chunk, core * WIDTH)],
            frames.at[chunk, rows_at(1 + 4 * core, 256, 4)],
            own_sem.at[chunk],
        )

    def remote(src, dst, send, recv, device):
        return pltpu.make_async_remote_copy(
            src_ref=src, dst_ref=dst, send_sem=send, recv_sem=recv, device_id=device, device_id_type=MESH
        )

    def core_copy(chunk):
        return remote(
            feat.at[:, cols(chunk, (1 - core) * WIDTH)],
            frames.at[chunk, rows_at(1 + 4 * core, 256, 4)],
            core_send.at[chunk],
            core_recv.at[chunk],
            place.other_core(),
        )

    def after_copy(chunk):
        return remote(
            frames.at[chunk, 2048:2304],
            frames.at[chunk, 0:256],
            after_send.at[chunk],
            after_recv.at[chunk],
            place.device(x + 1, y, z, core),
        )

    def before_copy(chunk):
        return remote(
            frames.at[chunk, 256:512],
            frames.at[chunk, 2304:2560],
            before_send.at[chunk],
            before_recv.at[chunk],
            place.device(x - 1, y, z, core),
        )

    def low_copy(chunk):
        return remote(
            recon.at[chunk, 384:576],
            recon.at[chunk, 0:192],
            low_send.at[chunk],
            low_recv.at[chunk],
            place.device(x + 1, y, z, core),
        )

    def high_copy(chunk):
        return remote(
            recon.at[chunk, 192:384],
            recon.at[chunk, 576:768],
            high_send.at[chunk],
            high_recv.at[chunk],
            place.device(x - 1, y, z, core),
        )

    def to_both_sides(up, down, act):
        @pl.when(inner_high)
        def _():
            act(up)

        @pl.when(inner_low)
        def _():
            act(down)

    def send_halo(chunk):
        to_both_sides(after_copy(chunk), before_copy(chunk), lambda copy: copy.start())

    def await_halo(chunk):
        to_both_sides(before_copy(chunk), after_copy(chunk), lambda copy: copy.wait_recv())

    def send_recon(chunk):
        to_both_sides(low_copy(chunk), high_copy(chunk), lambda copy: copy.start())

    def await_recon(chunk):
        to_both_sides(high_copy(chunk), low_copy(chunk), lambda copy: copy.wait_recv())

    for chunk in range(NCH):
        own_copy(chunk).start()

    barrier = pltpu.get_barrier_semaphore()
    partners = [place.other_core()]
    for axis in range(3):
        for step in (1, 2, 3):
            partners += [place.along(axis, step), place.along(axis, step, 1 - core)]
    for device in partners:
        pl.semaphore_signal(barrier, inc=1, device_id=device, device_id_type=MESH)
    pl.semaphore_wait(barrier, len(partners))

    for chunk in range(NCH):
        core_copy(chunk).start()

    @pl.when(clip_start)
    def _():
        for chunk in range(NCH):
            frames[chunk, 0:256] = jnp.zeros((256, SC), jnp.bfloat16)
            recon[chunk, 0:192] = jnp.zeros((192, SC), jnp.bfloat16)

    @pl.when(clip_end)
    def _():
        for chunk in range(NCH):
            frames[chunk, 2304:2560] = jnp.zeros((256, SC), jnp.bfloat16)
            recon[chunk, 576:768] = jnp.zeros((192, SC), jnp.bfloat16)

    ends = []
    for span in range(4):
        ends.append(spans[0, span] + (ends[-1] if ends else 0))

    def span_of(frame):
        return sum((frame >= end).astype(jnp.int32) for end in ends)

    def tap_mask(local, tap):
        frame = 8 * x + 1 + local
        same = (span_of(frame) == span_of(frame - tap)) & (frame >= tap) & (frame < 32)
        return jnp.where(same, 1.0, 0.0).astype(F32)

    def valid(local):
        frame = 8 * x + 1 + local
        return jnp.where((frame >= 0) & (frame < 32), 1.0, 0.0).astype(F32)

    row, column = (lax.broadcasted_iota(jnp.int32, (256, 256), axis) for axis in (0, 1))
    same = jnp.where(row == column, 1.0, 0.0).astype(jnp.bfloat16)
    for tap in range(3):
        block = 256 * (2 - tap)
        conv_t[block : block + 256] = dot_nt(same, conv_w[tap]).astype(jnp.bfloat16)
        second_t[256 * tap : 256 * tap + 256] = dot_nt(same, second_w[tap]).astype(jnp.bfloat16)

    for acc in (acc_second, acc_first, acc_out, acc_head):
        acc[...] = jnp.zeros_like(acc)

    head = head_w[...].astype(F32).reshape(1, 256)
    sign = (2 * labels[0] - 1).astype(F32)

    def positions(frame, chunk):
        return slice(frame * WIDTH + chunk * SC, frame * WIDTH + chunk * SC + SC)

    def turn(frame, chunk):
        turned[positions(frame, chunk)] = frames[chunk, rows_at(frame, 256)].T

    def activate(pre, center, slot, recon_slot, chunk):
        gate = 0.5 * jnp.tanh(0.5 * pre) + 0.5
        silu = pre * gate
        value = (turned[positions(center, chunk)].astype(F32) + silu).astype(jnp.bfloat16)
        hidden[positions(slot, chunk)] = value
        slopes[positions(slot, chunk)] = gate + silu * (1.0 - gate)
        recon[chunk, rows_at(recon_slot, 48)] = dot_nt(ow[...], value).astype(jnp.bfloat16)

    def decode(local, chunk):
        window = jnp.concatenate([turned[positions(local + tap, chunk)] for tap in range(3)], axis=1)
        weight = [
            conv_t[256 * block : 256 * block + 256]
            * jnp.full((1, 256), tap_mask(local, 2 - block), F32).astype(jnp.bfloat16)
            for block in range(3)
        ]
        pre = dot(window, jnp.concatenate(weight, axis=0))
        activate(pre, local + 2, local, local + 4, chunk)

    def await_frames(chunk):
        own_copy(chunk).wait()
        core_copy(chunk).wait_recv()

    def decode_inner(chunk):
        for frame in range(1, 9):
            turn(frame, chunk)
            if frame >= 3:
                decode(frame - 2, chunk)

        @pl.when(clip_start)
        def _():
            activate(dot(turned[positions(1, chunk)], conv_t[512:768]), 1, 8, 3, chunk)

    def decode_halo(chunk):
        await_halo(chunk)
        for frame in (0, 9):
            turn(frame, chunk)
        for local in (0, 7):
            decode(local, chunk)
        send_recon(chunk)

    def first_layer(local, chunk):
        pre = dot(recon[chunk, rows_at(local + 3, 48, 3)].T, fwt[...])
        if 0 <= local < 7:
            value = jnp.maximum(pre, 0.2 * pre)
        else:
            on = valid(local)
            value = pre * jnp.where(pre > 0, on, 0.2 * on)
        value = value.astype(jnp.bfloat16)
        disc[rows_at(local + 3, SC)] = value
        if -1 <= local < 9:
            disc_t[rows_at(local + 1, 256)] = value.T

    def second_layer(local):
        window = jnp.concatenate([disc[rows_at(local + 2 + tap, SC)] for tap in range(3)], axis=1)
        pre = dot(window, second_t[...])
        act = jnp.maximum(pre, 0.2 * pre)
        logits = jnp.sum(act * head, axis=1, keepdims=True)
        scale = -sign * loss_scale * (1.0 if 0 <= local < 7 else valid(local))
        signed = sign * logits
        small = jnp.exp(-jnp.abs(signed))
        one_over = pl.reciprocal(1.0 + small, approx=True)
        one_over = one_over * (2.0 - (1.0 + small) * one_over)
        grad = scale * jnp.where(signed > 0, small * one_over, one_over)
        if -1 <= local < 8:
            share = grad * jnp.where(clip_start, 1.0, 0.0).astype(F32) if local < 0 else grad
            acc_head[...] += jnp.sum((act * share).reshape(SC // 8, 8, 256), axis=0)
        second[rows_at(local + 2, SC)] = (jnp.where(pre > 0, head, 0.2 * head) * grad).astype(jnp.bfloat16)

    def first_back(local):
        window = jnp.concatenate([second[rows_at(local + 3 - tap, SC)] for tap in range(3)], axis=1)
        back = dot(window, second_w[...].reshape(768, 256))
        on = 1.0 if 0 <= local < 7 else valid(local)
        slope = jnp.where(disc[rows_at(local + 3, SC)].astype(F32) > 0, on, 0.2 * on)
        value = (back * slope).astype(jnp.bfloat16)
        first[rows_at(local + 1, SC)] = value
        parts[rows_at((local + 1) % 5, 144)] = dot_nt(fwt[...], value)

    def recon_back(local, where):
        total = (
            parts[pl.ds((local + 2) % 5 * 144, 48)]
            + parts[pl.ds((local + 1) % 5 * 144 + 48, 48)]
            + parts[pl.ds(local % 5 * 144 + 96, 48)]
        )
        rgrad[rows_at(local, 48), where] = total.astype(jnp.bfloat16)

    def recon_back_first(where):
        rgrad[rows_at(8, 48), where] = (parts[144:192] + parts[48:96]).astype(jnp.bfloat16)

    def wide(blocks):
        return jnp.concatenate(blocks, axis=1)

    def weight_grads(chunk):
        own, where = range(8), cols(chunk)
        left = wide([disc_t[t * 256 : t * 256 + 768] for t in own])
        acc_second[...] += dot(left, second[2 * SC : 10 * SC])
        left = wide([recon[chunk, (t + 3) * 48 : (t + 6) * 48] for t in own])
        acc_first[...] += dot(left, first[SC : 9 * SC])
        value = jnp.concatenate([hidden[positions(t, chunk)] for t in own], axis=0)
        acc_out[...] += dot(wide([rgrad[t * 48 : t * 48 + 48, where] for t in own]), value)

        @pl.when(clip_start)
        def _():
            acc_second[256:768] += dot(disc_t[0:512], second[SC : 2 * SC])
            acc_first[48:144] += dot(recon[chunk, 144:240], first[0:SC])
            acc_out[...] += dot(rgrad[384:432, where], hidden[positions(8, chunk)])

    await_frames(0)
    send_halo(0)
    decode_inner(0)
    decode_halo(0)
    for chunk in range(1, NCH):
        await_frames(chunk)
        decode_inner(chunk)

    for chunk in range(NCH):
        where = cols(chunk)
        await_recon(chunk)
        if chunk + 1 < NCH:
            send_halo(chunk + 1)
        for step in range(-3, 14):
            if step < 11:
                first_layer(step, chunk)
            if -2 <= step - 2 < 10:
                second_layer(step - 2)
            if -1 <= step - 4 < 9:
                first_back(step - 4)
            if step == 5:
                recon_back_first(where)
            if 0 <= step - 6:
                recon_back(step - 6, where)
        if chunk + 1 < NCH:
            decode_halo(chunk + 1)
        weight_grads(chunk)

    for part in range(3):
        grads1[part, 0:256] = acc_second[256 * part : 256 * part + 256].T
        grads1[part, 256:304] = acc_first[48 * part : 48 * part + 48]
        grads1[part, 304:320] = acc_out[16 * part : 16 * part + 16]
        grads1[part, 320:384] = jnp.zeros((64, 256), F32)
    grads1[0, 320:328] = jnp.broadcast_to(jnp.sum(acc_head[...], axis=0, keepdims=True), (8, 256))

    reduce1 = Reducer(place, grads1, total1, bufs[:3], send1, recv1)
    reduce2 = Reducer(place, grads2, total2, bufs[3:], send2, recv2)
    steps1, steps2 = reduce1.steps(), reduce2.steps()

    acc_conv = acc_second

    def conv_back(local):
        back = dot(rgrad[rows_at(local, 48)].T, ow[...])
        delta = (back * slopes[rows_at(local, WIDTH)]).astype(jnp.bfloat16)
        result = dot(wide([frames[chunk, rows_at(local, 256, 3)] for chunk in range(NCH)]), delta)
        for block, tap in ((0, 2), (1, 1), (2, 0)):
            rows = slice(256 * block, 256 * block + 256)
            term = result[rows] * tap_mask(local, tap)
            acc_conv[rows] = acc_conv[rows] + term if local else term

    def conv_back_first():
        back = dot(rgrad[rows_at(8, 48)].T, ow[...])
        delta = (back * slopes[rows_at(8, WIDTH)]).astype(jnp.bfloat16)
        acc_conv[512:768] += dot(wide([frames[chunk, 256:512] for chunk in range(NCH)]), delta)

    steps1[0]()
    for local in range(8):
        conv_back(local)
        if local == 0:
            pl.when(clip_start)(conv_back_first)
        if local == 5:
            steps1[1]()
    for tap in range(3):
        grads2[tap] = acc_conv[256 * (2 - tap) : 256 * (2 - tap) + 256].T
        reduce2.scatter_send(tap)
    steps1[2]()
    steps2[1]()
    steps1[3]()
    steps2[2]()
    steps1[4]()
    steps2[3]()
    steps2[4]()

    reduce1.finish()
    reduce2.finish()
    for chunk in range(NCH):
        core_copy(chunk).wait_send()

        to_both_sides(after_copy(chunk), before_copy(chunk), lambda copy: copy.wait_send())
        to_both_sides(low_copy(chunk), high_copy(chunk), lambda copy: copy.wait_send())


def per_device(
    features, conv_weight, out_weight, first_weight, second_weight, head_weight, span_lengths, labels
):
    clips, frame_count, channels, positions = features.shape
    total_count = (
        clips * lax.axis_size("dp") * lax.axis_size("group") * frame_count * lax.axis_size("tm") * positions
    )
    loss_scale = float(total_count) ** (-0.5)
    bf16 = jnp.bfloat16
    operands = (
        span_lengths,
        labels,
        features.reshape(frame_count * channels, positions),
        conv_weight,
        out_weight,
        jnp.swapaxes(first_weight, 1, 2).reshape(144, 256),
        second_weight,
        head_weight,
    )
    smem, vmem = pl.BlockSpec(memory_space=pltpu.SMEM), pl.BlockSpec(memory_space=pltpu.VMEM)
    dma = pltpu.SemaphoreType.DMA
    totals = pl.pallas_call(
        functools.partial(block_kernel, loss_scale),
        out_shape=(
            jax.ShapeDtypeStruct((3, 384, 256), bf16),
            jax.ShapeDtypeStruct((3, 256, 256), bf16),
        ),
        in_specs=[smem, smem, pl.BlockSpec(memory_space=pl.ANY)] + [vmem] * 5,
        out_specs=(vmem, vmem),
        scratch_shapes=[
            pltpu.VMEM((NCH, 2560, SC), bf16),
            pltpu.VMEM((10 * WIDTH, 256), bf16),
            pltpu.VMEM((9 * WIDTH, 256), bf16),
            pltpu.VMEM((9 * WIDTH, 256), F32),
            pltpu.VMEM((NCH, 768, SC), bf16),
            pltpu.VMEM((14 * SC, 256), bf16),
            pltpu.VMEM((10 * 256, SC), bf16),
            pltpu.VMEM((12 * SC, 256), bf16),
            pltpu.VMEM((10 * SC, 256), bf16),
            pltpu.VMEM((5 * 144, SC), F32),
            pltpu.VMEM((9 * 48, WIDTH), bf16),
            pltpu.VMEM((768, 256), bf16),
            pltpu.VMEM((768, 256), bf16),
            pltpu.VMEM((768, 256), F32),
            pltpu.VMEM((144, 256), F32),
            pltpu.VMEM((48, 256), F32),
            pltpu.VMEM((8, 256), F32),
            pltpu.VMEM((3, 384, 256), F32),
            pltpu.VMEM((3, 256, 256), F32),
            dma((NCH,)),
            dma((NCH,)),
            dma((NCH,)),
            dma((NCH,)),
            dma((NCH,)),
            dma((NCH,)),
            dma((NCH,)),
            dma((NCH,)),
            dma((NCH,)),
            dma((NCH,)),
            dma((NCH,)),
            dma((N_SLOTS,)),
            dma((N_SLOTS,)),
            dma((N_SLOTS,)),
            dma((N_SLOTS,)),
        ]
        + reduce_scratch(384)
        + reduce_scratch(256),
        compiler_params=pltpu.CompilerParams(
            collective_id=0, has_side_effects=True, vmem_limit_bytes=55 * MIB
        ),
    )(*operands)
    conv, out, first, second, head = pl.pallas_call(
        finish_kernel,
        out_shape=(
            jax.ShapeDtypeStruct((3, 256, 256), F32),
            jax.ShapeDtypeStruct((48, 256), F32),
            jax.ShapeDtypeStruct((3, 48, 256), F32),
            jax.ShapeDtypeStruct((3, 256, 256), F32),
            jax.ShapeDtypeStruct((1, 256), F32),
        ),
        in_specs=[vmem, vmem],
        out_specs=(vmem,) * 5,
        compiler_params=pltpu.CompilerParams(vmem_limit_bytes=16 * MIB),
    )(*totals)
    return conv, out, jnp.swapaxes(first, 1, 2), second, head.reshape(256)


def solution(mesh):
    placed = (
        P(("dp", "group"), "tm", None, None),
        P(),
        P(),
        P(),
        P(),
        P(),
        P(("dp", "group"), None),
        P(("dp", "group")),
    )
    return jax.shard_map(
        per_device, mesh=mesh, in_specs=placed, out_specs=(P(), P(), P(), P(), P()), check_vma=False
    )
```

```python
import functools

import jax
import jax.numpy as jnp
from jax import lax
from jax.experimental import pallas as pl
from jax.experimental.pallas import tpu as pltpu
from jax.sharding import PartitionSpec as P

MESH = pl.DeviceIdType.MESH
F32 = jnp.float32


class Place:
    def __init__(self):
        tm, dp, group = (lax.axis_index(name) for name in ("tm", "dp", "group"))
        self.core = lax.rem(tm, 2)
        self.at = (tm // 2, dp // 2, 2 * group + lax.rem(dp, 2))

    def device(self, x, y, z, core):
        return (2 * x + core, 2 * y + lax.rem(z, 2), z // 2)

    def along(self, axis, step, core=None):
        place = list(self.at)
        place[axis] = lax.rem(place[axis] + step, 4)
        return self.device(*place, self.core if core is None else core)

    def other_core(self):
        return self.device(*self.at, 1 - self.core)


class Reducer:
    def __init__(self, place, grads, total, first_row, bufs, send_sems, recv_sems):
        self.place, self.grads, self.total, self.first_row = (place, grads, total, first_row)
        self.in1, self.in2, self.in3 = bufs
        self.send_sems, self.recv_sems = (send_sems, recv_sems)
        self.size = grads.shape[1] // 8
        self.sent = []

    def axis(self, part, level):
        return (part + level) % 3

    def copy(self, src, dst, slot, device):
        return pltpu.make_async_remote_copy(
            src_ref=src,
            dst_ref=dst,
            send_sem=self.send_sems.at[slot],
            recv_sem=self.recv_sems.at[slot],
            device_id=device,
            device_id_type=MESH,
        )

    def start(self, *args):
        copy = self.copy(*args)
        copy.start()
        self.sent.append(copy)

    def await_copy(self, ref, slot):
        self.copy(ref, ref, slot, self.place.other_core()).wait_recv()

    def index(self, part):
        return 2 * self.place.at[self.axis(part, 0)] + self.place.core

    def block(self, index):
        return pl.ds(pl.multiple_of(index * self.size, self.size), self.size)

    def result_block(self, part):
        return pl.ds(pl.multiple_of(self.first_row + self.index(part) * self.size, 16), self.size)

    def member(self, part, index):
        place = list(self.place.at)
        place[self.axis(part, 0)] = index // 2
        return self.place.device(*place, lax.rem(index, 2))

    def scatter_send(self, part):
        for step in range(1, 8):
            target = lax.rem(self.index(part) + step, 8)
            src = self.grads.at[part, self.block(target)]
            self.start(src, self.in1.at[part, step - 1], 20 * part + step - 1, self.member(part, target))

    def scatter_sum(self, part):
        for step in range(1, 8):
            self.await_copy(self.in1.at[part, step - 1], 20 * part + step - 1)
        result = self.grads[part, self.block(self.index(part))]
        for step in range(1, 8):
            result = result + self.in1[part, step - 1]
        self.in2[part, self.place.at[self.axis(part, 1)]] = result

    def swap_send(self, part, level):
        axis = self.axis(part, level)
        here = (self.in2, self.in3)[level - 1].at[part, self.place.at[axis]]
        for step in (1, 2, 3):
            self.start(here, here, 20 * part + 3 + 3 * level + step, self.place.along(axis, step))

    def swap_sum(self, part, level):
        held = (self.in2, self.in3)[level - 1]
        for step in (1, 2, 3):
            self.await_copy(held.at[part, step], 20 * part + 3 + 3 * level + step)
        result = (held[part, 0] + held[part, 1]) + (held[part, 2] + held[part, 3])
        if level == 1:
            self.in3[part, self.place.at[self.axis(part, 2)]] = result
        else:
            self.total[part, self.result_block(part)] = result.astype(self.total.dtype)

    def gather_send(self, part):
        here = self.total.at[part, self.result_block(part)]
        for step in range(1, 8):
            target = lax.rem(self.index(part) + step, 8)
            self.start(here, here, 20 * part + 12 + step, self.member(part, target))

    def gather_wait(self, part):
        here = self.total.at[part, self.result_block(part)]
        for step in range(1, 8):
            self.await_copy(here, 20 * part + 12 + step)

    def steps(self):
        def each(*calls):
            def run():
                for part in range(3):
                    for call, *level in calls:
                        call(part, *level)

            return run

        return [
            each((self.scatter_send,)),
            each((self.scatter_sum,), (self.swap_send, 1)),
            each((self.swap_sum, 1), (self.swap_send, 2)),
            each((self.swap_sum, 2), (self.gather_send,)),
            each((self.gather_wait,)),
        ]

    def finish(self):
        for copy in self.sent:
            copy.wait_send()


N_SLOTS = 60


def reduce_scratch(rows):
    size = rows // 8
    return [
        pltpu.VMEM((3, 7, size, 256), F32),
        pltpu.VMEM((3, 4, size, 256), F32),
        pltpu.VMEM((3, 4, size, 256), F32),
    ]


SC = 512
WIDTH = 1024
NCH = WIDTH // SC
MIB = 1024 * 1024


def dot(a, b):
    return jnp.dot(a, b, preferred_element_type=F32)


def dot_nt(a, b):
    return lax.dot_general(a, b, (((1,), (1,)), ((), ())), preferred_element_type=F32)


def rows_at(frame, height, count=1):
    start = frame * height
    return pl.ds(start if isinstance(start, int) else pl.multiple_of(start, height), height * count)


def finish_kernel(total, conv_out, out_out, first_out, second_out, head_out):
    for part in range(3):
        conv_out[part] = total[part, 384:640].astype(F32)
        second_out[part] = total[part, 0:256].astype(F32)
        first_out[part] = total[part, 256:304].astype(F32)
        out_out[16 * part : 16 * part + 16] = total[part, 304:320].astype(F32)
    head_out[...] = total[0, 320:336].astype(F32)[0:1]


def block_kernel(
    loss_scale,
    spans, labels, feat, conv_w, ow, fwt, second_w, head_w,
    total,
    frames, turned, hidden, slopes, recon, disc, disc_t, second, first, parts, rgrad, conv_t, second_t,
    acc_second, acc_first, acc_out, acc_head, grads1, grads2,
    own_sem, core_send, core_recv, after_send, after_recv, before_send, before_recv,
    low_send, low_recv, high_send, high_recv,
    send1, recv1, send2, recv2, *bufs,
):
    place = Place()
    x, y, z = place.at
    core = place.core
    clip_start, clip_end = x == 0, x == 3
    inner_low, inner_high = x > 0, x < 3

    def cols(chunk, base=0):
        return pl.ds(pl.multiple_of(base + chunk * SC, SC), SC)

    def own_copy(chunk):
        return pltpu.make_async_copy(
            feat.at[:, cols(chunk, core * WIDTH)],
            frames.at[chunk, rows_at(1 + 4 * core, 256, 4)],
            own_sem.at[chunk],
        )

    def remote(src, dst, send, recv, device):
        return pltpu.make_async_remote_copy(
            src_ref=src, dst_ref=dst, send_sem=send, recv_sem=recv, device_id=device, device_id_type=MESH
        )

    def core_copy(chunk):
        return remote(
            feat.at[:, cols(chunk, (1 - core) * WIDTH)],
            frames.at[chunk, rows_at(1 + 4 * core, 256, 4)],
            core_send.at[chunk],
            core_recv.at[chunk],
            place.other_core(),
        )

    def after_copy(chunk, target):
        return remote(
            feat.at[768:1024, cols(chunk, target * WIDTH)],
            frames.at[chunk, 0:256],
            after_send.at[chunk, target],
            after_recv.at[chunk],
            place.device(x + 1, y, z, target),
        )

    def before_copy(chunk, target):
        return remote(
            feat.at[0:256, cols(chunk, target * WIDTH)],
            frames.at[chunk, 2304:2560],
            before_send.at[chunk, target],
            before_recv.at[chunk],
            place.device(x - 1, y, z, target),
        )

    def low_copy(chunk):
        return remote(
            recon.at[chunk, 384:576],
            recon.at[chunk, 0:192],
            low_send.at[chunk],
            low_recv.at[chunk],
            place.device(x + 1, y, z, core),
        )

    def high_copy(chunk):
        return remote(
            recon.at[chunk, 192:384],
            recon.at[chunk, 576:768],
            high_send.at[chunk],
            high_recv.at[chunk],
            place.device(x - 1, y, z, core),
        )

    def to_both_sides(up, down, act):
        @pl.when(inner_high)
        def _():
            act(up)

        @pl.when(inner_low)
        def _():
            act(down)

    def each_halo(chunk, act):
        @pl.when((core == 1) & inner_high)
        def _():
            for target in (0, 1):
                act(after_copy(chunk, target))

        @pl.when((core == 0) & inner_low)
        def _():
            for target in (0, 1):
                act(before_copy(chunk, target))

    def send_halo(chunk):
        each_halo(chunk, lambda copy: copy.start())

    def await_halo(chunk):
        to_both_sides(before_copy(chunk, 0), after_copy(chunk, 0), lambda copy: copy.wait_recv())

    def send_recon(chunk):
        to_both_sides(low_copy(chunk), high_copy(chunk), lambda copy: copy.start())

    def await_recon(chunk):
        to_both_sides(high_copy(chunk), low_copy(chunk), lambda copy: copy.wait_recv())

    for chunk in range(NCH):
        own_copy(chunk).start()

    barrier = pltpu.get_barrier_semaphore()
    partners = [place.other_core()]
    for axis in range(3):
        for step in (1, 2, 3):
            partners += [place.along(axis, step), place.along(axis, step, 1 - core)]
    for device in partners:
        pl.semaphore_signal(barrier, inc=1, device_id=device, device_id_type=MESH)
    pl.semaphore_wait(barrier, len(partners))

    send_halo(0)
    for chunk in range(NCH):
        core_copy(chunk).start()

    @pl.when(clip_start)
    def _():
        for chunk in range(NCH):
            frames[chunk, 0:256] = jnp.zeros((256, SC), jnp.bfloat16)
            recon[chunk, 0:192] = jnp.zeros((192, SC), jnp.bfloat16)

    @pl.when(clip_end)
    def _():
        for chunk in range(NCH):
            frames[chunk, 2304:2560] = jnp.zeros((256, SC), jnp.bfloat16)
            recon[chunk, 576:768] = jnp.zeros((192, SC), jnp.bfloat16)

    ends = []
    for span in range(4):
        ends.append(spans[0, span] + (ends[-1] if ends else 0))

    def span_of(frame):
        return sum((frame >= end).astype(jnp.int32) for end in ends)

    def tap_mask(local, tap):
        frame = 8 * x + 1 + local
        same = (span_of(frame) == span_of(frame - tap)) & (frame >= tap) & (frame < 32)
        return jnp.where(same, 1.0, 0.0).astype(F32)

    def valid(local):
        frame = 8 * x + 1 + local
        return jnp.where((frame >= 0) & (frame < 32), 1.0, 0.0).astype(F32)

    row, column = (lax.broadcasted_iota(jnp.int32, (256, 256), axis) for axis in (0, 1))
    same = jnp.where(row == column, 1.0, 0.0).astype(jnp.bfloat16)
    for tap in range(3):
        block = 256 * (2 - tap)
        conv_t[block : block + 256] = dot_nt(same, conv_w[tap]).astype(jnp.bfloat16)
        second_t[256 * tap : 256 * tap + 256] = dot_nt(same, second_w[tap]).astype(jnp.bfloat16)

    for acc in (acc_second, acc_first, acc_out, acc_head):
        acc[...] = jnp.zeros_like(acc)

    head = head_w[...].astype(F32)
    sign = (2 * labels[0] - 1).astype(F32)

    def positions(frame, chunk):
        start = frame * WIDTH + chunk * SC
        return slice(start, start + SC) if isinstance(start, int) else pl.ds(pl.multiple_of(start, SC), SC)

    def turn(frame, chunk):
        turned[positions(frame, chunk)] = frames[chunk, rows_at(frame, 256)].T

    def activate(pre, center, slot, recon_slot, chunk):
        gate = 0.5 * jnp.tanh(0.5 * pre) + 0.5
        silu = pre * gate
        value = (turned[positions(center, chunk)].astype(F32) + silu).astype(jnp.bfloat16)
        hidden[positions(slot, chunk)] = value
        slopes[positions(slot, chunk)] = gate + silu * (1.0 - gate)
        recon[chunk, rows_at(recon_slot, 48)] = dot_nt(ow[...], value).astype(jnp.bfloat16)

    def decode(local, chunk):
        window = jnp.concatenate([turned[positions(local + tap, chunk)] for tap in range(3)], axis=1)
        weight = [
            conv_t[256 * block : 256 * block + 256]
            * jnp.full((1, 256), tap_mask(local, 2 - block), F32).astype(jnp.bfloat16)
            for block in range(3)
        ]
        pre = dot(window, jnp.concatenate(weight, axis=0))
        activate(pre, local + 2, local, local + 4, chunk)

    def decode_inner(chunk):
        mine, other = 1 + 4 * core, 5 - 4 * core
        own_copy(chunk).wait()
        for offset in range(4):
            turn(mine + offset, chunk)
        decode(mine, chunk)
        decode(mine + 1, chunk)
        core_copy(chunk).wait_recv()
        for offset in range(4):
            turn(other + offset, chunk)
        for local in (3, 4, other, other + 1):
            decode(local, chunk)

        @pl.when(clip_start)
        def _():
            activate(dot(turned[positions(1, chunk)], conv_t[512:768]), 1, 8, 3, chunk)

    def decode_halo(chunk):
        await_halo(chunk)
        for frame in (0, 9):
            turn(frame, chunk)
        for local in (0, 7):
            decode(local, chunk)
        send_recon(chunk)

    def first_layer(local, chunk):
        pre = dot(recon[chunk, rows_at(local + 3, 48, 3)].T, fwt[...])
        if 0 <= local < 7:
            value = jnp.maximum(pre, 0.2 * pre)
        else:
            on = valid(local)
            value = pre * jnp.where(pre > 0, on, 0.2 * on)
        value = value.astype(jnp.bfloat16)
        disc[rows_at(local + 3, SC)] = value
        if -1 <= local < 9:
            disc_t[rows_at(local + 1, 256)] = value.T

    def second_layer(local):
        window = jnp.concatenate([disc[rows_at(local + 2 + tap, SC)] for tap in range(3)], axis=1)
        pre = dot(window, second_t[...])
        act = jnp.maximum(pre, 0.2 * pre)
        logits = jnp.sum(act * head, axis=1, keepdims=True)
        scale = -sign * loss_scale * (1.0 if 0 <= local < 7 else valid(local))
        signed = sign * logits
        small = jnp.exp(-jnp.abs(signed))
        one_over = pl.reciprocal(1.0 + small, approx=True)
        one_over = one_over * (2.0 - (1.0 + small) * one_over)
        grad = scale * jnp.where(signed > 0, small * one_over, one_over)
        if -1 <= local < 8:
            share = grad * jnp.where(clip_start, 1.0, 0.0).astype(F32) if local < 0 else grad
            acc_head[...] += jnp.sum((act * share).reshape(SC // 8, 8, 256), axis=0)
        second[rows_at(local + 2, SC)] = (jnp.where(pre > 0, head, 0.2 * head) * grad).astype(jnp.bfloat16)

    def first_back(local):
        window = jnp.concatenate([second[rows_at(local + 3 - tap, SC)] for tap in range(3)], axis=1)
        back = dot(window, second_w[...].reshape(768, 256))
        on = 1.0 if 0 <= local < 7 else valid(local)
        slope = jnp.where(disc[rows_at(local + 3, SC)].astype(F32) > 0, on, 0.2 * on)
        value = (back * slope).astype(jnp.bfloat16)
        first[rows_at(local + 1, SC)] = value
        parts[rows_at((local + 1) % 5, 144)] = dot_nt(fwt[...], value)

    def recon_back(local, where):
        total = (
            parts[pl.ds((local + 2) % 5 * 144, 48)]
            + parts[pl.ds((local + 1) % 5 * 144 + 48, 48)]
            + parts[pl.ds(local % 5 * 144 + 96, 48)]
        )
        rgrad[rows_at(local, 48), where] = total.astype(jnp.bfloat16)

    def recon_back_first(where):
        rgrad[rows_at(8, 48), where] = (parts[144:192] + parts[48:96]).astype(jnp.bfloat16)

    def wide(blocks):
        return jnp.concatenate(blocks, axis=1)

    def weight_grads(chunk):
        own, where = range(8), cols(chunk)
        left = wide([disc_t[t * 256 : t * 256 + 768] for t in own])
        acc_second[...] += dot(left, second[2 * SC : 10 * SC])
        left = wide([recon[chunk, (t + 3) * 48 : (t + 6) * 48] for t in own])
        acc_first[...] += dot(left, first[SC : 9 * SC])
        value = jnp.concatenate([hidden[positions(t, chunk)] for t in own], axis=0)
        acc_out[...] += dot(wide([rgrad[t * 48 : t * 48 + 48, where] for t in own]), value)

        @pl.when(clip_start)
        def _():
            acc_second[256:768] += dot(disc_t[0:512], second[SC : 2 * SC])
            acc_first[48:144] += dot(recon[chunk, 144:240], first[0:SC])
            acc_out[...] += dot(rgrad[384:432, where], hidden[positions(8, chunk)])

    decode_inner(0)
    decode_halo(0)
    for chunk in range(1, NCH):
        decode_inner(chunk)

    for chunk in range(NCH):
        where = cols(chunk)
        await_recon(chunk)
        if chunk + 1 < NCH:
            send_halo(chunk + 1)
        for step in range(-3, 14):
            if step < 11:
                first_layer(step, chunk)
            if -2 <= step - 2 < 10:
                second_layer(step - 2)
            if -1 <= step - 4 < 9:
                first_back(step - 4)
            if step == 5:
                recon_back_first(where)
            if 0 <= step - 6:
                recon_back(step - 6, where)
        if chunk + 1 < NCH:
            decode_halo(chunk + 1)
        weight_grads(chunk)

    for part in range(3):
        grads1[part, 0:256] = acc_second[256 * part : 256 * part + 256].T
        grads1[part, 256:304] = acc_first[48 * part : 48 * part + 48]
        grads1[part, 304:320] = acc_out[16 * part : 16 * part + 16]
        grads1[part, 320:384] = jnp.zeros((64, 256), F32)
    grads1[0, 320:328] = jnp.broadcast_to(jnp.sum(acc_head[...], axis=0, keepdims=True), (8, 256))

    reduce1 = Reducer(place, grads1, total, 0, bufs[:3], send1, recv1)
    reduce2 = Reducer(place, grads2, total, 384, bufs[3:], send2, recv2)
    steps1, steps2 = reduce1.steps(), reduce2.steps()

    acc_conv = acc_second

    def conv_back(local):
        back = dot(rgrad[rows_at(local, 48)].T, ow[...])
        delta = (back * slopes[rows_at(local, WIDTH)]).astype(jnp.bfloat16)
        result = dot(wide([frames[chunk, rows_at(local, 256, 3)] for chunk in range(NCH)]), delta)
        for block, tap in ((0, 2), (1, 1), (2, 0)):
            rows = slice(256 * block, 256 * block + 256)
            term = result[rows] * tap_mask(local, tap)
            acc_conv[rows] = acc_conv[rows] + term if local else term

    def conv_back_first():
        back = dot(rgrad[rows_at(8, 48)].T, ow[...])
        delta = (back * slopes[rows_at(8, WIDTH)]).astype(jnp.bfloat16)
        acc_conv[512:768] += dot(wide([frames[chunk, 256:512] for chunk in range(NCH)]), delta)

    steps1[0]()
    for local in range(8):
        conv_back(local)
        if local == 0:
            pl.when(clip_start)(conv_back_first)
        if local == 5:
            steps1[1]()
    for tap in range(3):
        grads2[tap] = acc_conv[256 * (2 - tap) : 256 * (2 - tap) + 256].T
        reduce2.scatter_send(tap)
    steps1[2]()
    steps2[1]()
    steps1[3]()
    steps2[2]()
    steps1[4]()
    steps2[3]()
    steps2[4]()

    reduce1.finish()
    reduce2.finish()
    for chunk in range(NCH):
        core_copy(chunk).wait_send()

        each_halo(chunk, lambda copy: copy.wait_send())
        to_both_sides(low_copy(chunk), high_copy(chunk), lambda copy: copy.wait_send())


def per_device(
    features, conv_weight, out_weight, first_weight, second_weight, head_weight, span_lengths, labels
):
    clips, frame_count, channels, positions = features.shape
    total_count = (
        clips * lax.axis_size("dp") * lax.axis_size("group") * frame_count * lax.axis_size("tm") * positions
    )
    loss_scale = float(total_count) ** (-0.5)
    bf16 = jnp.bfloat16
    operands = (
        span_lengths,
        labels,
        features.reshape(frame_count * channels, positions),
        conv_weight,
        out_weight,
        jnp.swapaxes(first_weight, 1, 2).reshape(144, 256),
        second_weight,
        head_weight.reshape(1, 256),
    )
    smem, vmem = pl.BlockSpec(memory_space=pltpu.SMEM), pl.BlockSpec(memory_space=pltpu.VMEM)
    dma = pltpu.SemaphoreType.DMA
    total = pl.pallas_call(
        functools.partial(block_kernel, loss_scale),
        out_shape=jax.ShapeDtypeStruct((3, 640, 256), bf16),
        in_specs=[smem, smem, pl.BlockSpec(memory_space=pl.ANY)] + [vmem] * 5,
        out_specs=vmem,
        scratch_shapes=[
            pltpu.VMEM((NCH, 2560, SC), bf16),
            pltpu.VMEM((10 * WIDTH, 256), bf16),
            pltpu.VMEM((9 * WIDTH, 256), bf16),
            pltpu.VMEM((9 * WIDTH, 256), F32),
            pltpu.VMEM((NCH, 768, SC), bf16),
            pltpu.VMEM((14 * SC, 256), bf16),
            pltpu.VMEM((10 * 256, SC), bf16),
            pltpu.VMEM((12 * SC, 256), bf16),
            pltpu.VMEM((10 * SC, 256), bf16),
            pltpu.VMEM((5 * 144, SC), F32),
            pltpu.VMEM((9 * 48, WIDTH), bf16),
            pltpu.VMEM((768, 256), bf16),
            pltpu.VMEM((768, 256), bf16),
            pltpu.VMEM((768, 256), F32),
            pltpu.VMEM((144, 256), F32),
            pltpu.VMEM((48, 256), F32),
            pltpu.VMEM((8, 256), F32),
            pltpu.VMEM((3, 384, 256), F32),
            pltpu.VMEM((3, 256, 256), F32),
            dma((NCH,)),
            dma((NCH,)),
            dma((NCH,)),
            dma((NCH, 2)),
            dma((NCH,)),
            dma((NCH, 2)),
            dma((NCH,)),
            dma((NCH,)),
            dma((NCH,)),
            dma((NCH,)),
            dma((NCH,)),
            dma((N_SLOTS,)),
            dma((N_SLOTS,)),
            dma((N_SLOTS,)),
            dma((N_SLOTS,)),
        ]
        + reduce_scratch(384)
        + reduce_scratch(256),
        compiler_params=pltpu.CompilerParams(
            collective_id=0, has_side_effects=True, vmem_limit_bytes=55 * MIB
        ),
    )(*operands)
    conv, out, first, second, head = pl.pallas_call(
        finish_kernel,
        out_shape=(
            jax.ShapeDtypeStruct((3, 256, 256), F32),
            jax.ShapeDtypeStruct((48, 256), F32),
            jax.ShapeDtypeStruct((3, 48, 256), F32),
            jax.ShapeDtypeStruct((3, 256, 256), F32),
            jax.ShapeDtypeStruct((1, 256), F32),
        ),
        in_specs=[vmem],
        out_specs=(vmem,) * 5,
        compiler_params=pltpu.CompilerParams(vmem_limit_bytes=16 * MIB),
    )(total)
    return conv, out, jnp.swapaxes(first, 1, 2), second, head.reshape(256)


def solution(mesh):
    placed = (
        P(("dp", "group"), "tm", None, None),
        P(),
        P(),
        P(),
        P(),
        P(),
        P(("dp", "group"), None),
        P(("dp", "group")),
    )
    return jax.shard_map(
        per_device, mesh=mesh, in_specs=placed, out_specs=(P(), P(), P(), P(), P()), check_vma=False
    )
```

```python
import functools

import jax
import jax.numpy as jnp
from jax import lax
from jax.experimental import pallas as pl
from jax.experimental.pallas import tpu as pltpu
from jax.sharding import PartitionSpec as P

MESH = pl.DeviceIdType.MESH
F32 = jnp.float32


class Place:
    def __init__(self):
        tm, dp, group = (lax.axis_index(name) for name in ("tm", "dp", "group"))
        self.core = lax.rem(tm, 2)
        self.at = (tm // 2, dp // 2, 2 * group + lax.rem(dp, 2))

    def device(self, x, y, z, core):
        return (2 * x + core, 2 * y + lax.rem(z, 2), z // 2)

    def along(self, axis, step, core=None):
        place = list(self.at)
        place[axis] = lax.rem(place[axis] + step, 4)
        return self.device(*place, self.core if core is None else core)

    def other_core(self):
        return self.device(*self.at, 1 - self.core)


class Reducer:
    def __init__(self, place, grads, total, first_row, bufs, send_sems, recv_sems):
        self.place, self.grads, self.total, self.first_row = (place, grads, total, first_row)
        self.in1, self.in2, self.in3 = bufs
        self.send_sems, self.recv_sems = (send_sems, recv_sems)
        self.size = grads.shape[1] // 8
        self.sent = []

    def axis(self, part, level):
        return (part + level) % 3

    def copy(self, src, dst, slot, device):
        return pltpu.make_async_remote_copy(
            src_ref=src,
            dst_ref=dst,
            send_sem=self.send_sems.at[slot],
            recv_sem=self.recv_sems.at[slot],
            device_id=device,
            device_id_type=MESH,
        )

    def start(self, *args):
        copy = self.copy(*args)
        copy.start()
        self.sent.append(copy)

    def await_copy(self, ref, slot):
        self.copy(ref, ref, slot, self.place.other_core()).wait_recv()

    def index(self, part):
        return 2 * self.place.at[self.axis(part, 0)] + self.place.core

    def block(self, index):
        return pl.ds(pl.multiple_of(index * self.size, self.size), self.size)

    def result_block(self, part):
        return pl.ds(pl.multiple_of(self.first_row + self.index(part) * self.size, 16), self.size)

    def member(self, part, index):
        place = list(self.place.at)
        place[self.axis(part, 0)] = index // 2
        return self.place.device(*place, lax.rem(index, 2))

    def scatter_send(self, part):
        for step in range(1, 8):
            target = lax.rem(self.index(part) + step, 8)
            src = self.grads.at[part, self.block(target)]
            self.start(src, self.in1.at[part, step - 1], 20 * part + step - 1, self.member(part, target))

    def scatter_sum(self, part):
        for step in range(1, 8):
            self.await_copy(self.in1.at[part, step - 1], 20 * part + step - 1)
        result = self.grads[part, self.block(self.index(part))]
        for step in range(1, 8):
            result = result + self.in1[part, step - 1]
        self.in2[part, self.place.at[self.axis(part, 1)]] = result

    def swap_send(self, part, level):
        axis = self.axis(part, level)
        here = (self.in2, self.in3)[level - 1].at[part, self.place.at[axis]]
        for step in (1, 2, 3):
            self.start(here, here, 20 * part + 3 + 3 * level + step, self.place.along(axis, step))

    def swap_sum(self, part, level):
        held = (self.in2, self.in3)[level - 1]
        for step in (1, 2, 3):
            self.await_copy(held.at[part, step], 20 * part + 3 + 3 * level + step)
        result = (held[part, 0] + held[part, 1]) + (held[part, 2] + held[part, 3])
        if level == 1:
            self.in3[part, self.place.at[self.axis(part, 2)]] = result
        else:
            self.total[part, self.result_block(part)] = result.astype(self.total.dtype)

    def gather_send(self, part):
        here = self.total.at[part, self.result_block(part)]
        for step in range(1, 8):
            target = lax.rem(self.index(part) + step, 8)
            self.start(here, here, 20 * part + 12 + step, self.member(part, target))

    def gather_wait(self, part):
        here = self.total.at[part, self.result_block(part)]
        for step in range(1, 8):
            self.await_copy(here, 20 * part + 12 + step)

    def steps(self):
        def each(*calls):
            def run():
                for part in range(3):
                    for call, *level in calls:
                        call(part, *level)

            return run

        return [
            each((self.scatter_send,)),
            each((self.scatter_sum,), (self.swap_send, 1)),
            each((self.swap_sum, 1), (self.swap_send, 2)),
            each((self.swap_sum, 2), (self.gather_send,)),
            each((self.gather_wait,)),
        ]

    def finish(self):
        for copy in self.sent:
            copy.wait_send()


N_SLOTS = 60


def reduce_scratch(rows):
    size = rows // 8
    return [
        pltpu.VMEM((3, 7, size, 256), F32),
        pltpu.VMEM((3, 4, size, 256), F32),
        pltpu.VMEM((3, 4, size, 256), F32),
    ]


SC = 512
WIDTH = 1024
NCH = WIDTH // SC
MIB = 1024 * 1024


def dot(a, b):
    return jnp.dot(a, b, preferred_element_type=F32)


def dot_nt(a, b):
    return lax.dot_general(a, b, (((1,), (1,)), ((), ())), preferred_element_type=F32)


def rows_at(frame, height, count=1):
    start = frame * height
    return pl.ds(start if isinstance(start, int) else pl.multiple_of(start, height), height * count)


def finish_kernel(total, conv_out, out_out, first_out, second_out, head_out):
    for part in range(3):
        conv_out[part] = total[part, 384:640].astype(F32)
        second_out[part] = total[part, 0:256].astype(F32)
        first_out[part] = total[part, 256:304].astype(F32)
        out_out[16 * part : 16 * part + 16] = total[part, 304:320].astype(F32)
    head_out[...] = total[0, 320:336].astype(F32)[0:1]


def block_kernel(
    loss_scale,
    spans, labels, feat, conv_w, ow, fwt, second_w, head_w,
    total,
    frames, turned, hidden, slopes, recon, disc, disc_t, second, first, parts, rgrad, conv_t, second_t,
    acc_second, acc_first, acc_out, acc_head, grads1, grads2,
    own_sem, core_send, core_recv, after_send, after_recv, before_send, before_recv,
    low_send, low_recv, high_send, high_recv,
    send1, recv1, send2, recv2, *bufs,
):
    place = Place()
    x, y, z = place.at
    core = place.core
    clip_start, clip_end = x == 0, x == 3
    inner_low, inner_high = x > 0, x < 3

    def cols(chunk, base=0):
        return pl.ds(pl.multiple_of(base + chunk * SC, SC), SC)

    def own_copy(chunk):
        return pltpu.make_async_copy(
            feat.at[:, cols(chunk, core * WIDTH)],
            frames.at[chunk, rows_at(1 + 4 * core, 256, 4)],
            own_sem.at[chunk],
        )

    def remote(src, dst, send, recv, device):
        return pltpu.make_async_remote_copy(
            src_ref=src, dst_ref=dst, send_sem=send, recv_sem=recv, device_id=device, device_id_type=MESH
        )

    def core_copy(chunk):
        return remote(
            feat.at[:, cols(chunk, (1 - core) * WIDTH)],
            frames.at[chunk, rows_at(1 + 4 * core, 256, 4)],
            core_send.at[chunk],
            core_recv.at[chunk],
            place.other_core(),
        )

    def after_copy(chunk, target):
        return remote(
            feat.at[768:1024, cols(chunk, target * WIDTH)],
            frames.at[chunk, 0:256],
            after_send.at[chunk, target],
            after_recv.at[chunk],
            place.device(x + 1, y, z, target),
        )

    def before_copy(chunk, target):
        return remote(
            feat.at[0:256, cols(chunk, target * WIDTH)],
            frames.at[chunk, 2304:2560],
            before_send.at[chunk, target],
            before_recv.at[chunk],
            place.device(x - 1, y, z, target),
        )

    def low_copy(chunk):
        return remote(
            recon.at[chunk, 384:576],
            recon.at[chunk, 0:192],
            low_send.at[chunk],
            low_recv.at[chunk],
            place.device(x + 1, y, z, core),
        )

    def high_copy(chunk):
        return remote(
            recon.at[chunk, 192:384],
            recon.at[chunk, 576:768],
            high_send.at[chunk],
            high_recv.at[chunk],
            place.device(x - 1, y, z, core),
        )

    def to_both_sides(up, down, act):
        @pl.when(inner_high)
        def _():
            act(up)

        @pl.when(inner_low)
        def _():
            act(down)

    def each_halo(chunk, act):
        @pl.when((core == 1) & inner_high)
        def _():
            for target in (0, 1):
                act(after_copy(chunk, target))

        @pl.when((core == 0) & inner_low)
        def _():
            for target in (0, 1):
                act(before_copy(chunk, target))

    def send_halo(chunk):
        each_halo(chunk, lambda copy: copy.start())

    def await_halo(chunk):
        to_both_sides(before_copy(chunk, 0), after_copy(chunk, 0), lambda copy: copy.wait_recv())

    def send_recon(chunk):
        to_both_sides(low_copy(chunk), high_copy(chunk), lambda copy: copy.start())

    def await_recon(chunk):
        to_both_sides(high_copy(chunk), low_copy(chunk), lambda copy: copy.wait_recv())

    for chunk in range(NCH):
        own_copy(chunk).start()

    barrier = pltpu.get_barrier_semaphore()
    partners = [place.other_core()]
    for axis in range(3):
        for step in (1, 2, 3):
            partners += [place.along(axis, step), place.along(axis, step, 1 - core)]
    for device in partners:
        pl.semaphore_signal(barrier, inc=1, device_id=device, device_id_type=MESH)
    pl.semaphore_wait(barrier, len(partners))

    send_halo(0)
    for chunk in range(NCH):
        core_copy(chunk).start()

    @pl.when(clip_start)
    def _():
        for chunk in range(NCH):
            frames[chunk, 0:256] = jnp.zeros((256, SC), jnp.bfloat16)
            recon[chunk, 0:192] = jnp.zeros((192, SC), jnp.bfloat16)

    @pl.when(clip_end)
    def _():
        for chunk in range(NCH):
            frames[chunk, 2304:2560] = jnp.zeros((256, SC), jnp.bfloat16)
            recon[chunk, 576:768] = jnp.zeros((192, SC), jnp.bfloat16)

    ends = []
    for span in range(4):
        ends.append(spans[0, span] + (ends[-1] if ends else 0))

    def span_of(frame):
        return sum((frame >= end).astype(jnp.int32) for end in ends)

    def tap_mask(local, tap):
        frame = 8 * x + 1 + local
        same = (span_of(frame) == span_of(frame - tap)) & (frame >= tap) & (frame < 32)
        return jnp.where(same, 1.0, 0.0).astype(F32)

    def valid(local):
        frame = 8 * x + 1 + local
        return jnp.where((frame >= 0) & (frame < 32), 1.0, 0.0).astype(F32)

    row, column = (lax.broadcasted_iota(jnp.int32, (256, 256), axis) for axis in (0, 1))
    same = jnp.where(row == column, 1.0, 0.0).astype(jnp.bfloat16)
    for tap in range(3):
        block = 256 * (2 - tap)
        conv_t[block : block + 256] = dot_nt(same, conv_w[tap]).astype(jnp.bfloat16)
        second_t[256 * tap : 256 * tap + 256] = dot_nt(same, second_w[tap]).astype(jnp.bfloat16)

    for acc in (acc_second, acc_first, acc_out, acc_head):
        acc[...] = jnp.zeros_like(acc)

    head = head_w[...].astype(F32)
    sign = (2 * labels[0] - 1).astype(F32)

    def positions(frame, chunk):
        start = frame * WIDTH + chunk * SC
        return slice(start, start + SC) if isinstance(start, int) else pl.ds(pl.multiple_of(start, SC), SC)

    def turn(frame, chunk):
        turned[positions(frame, chunk)] = frames[chunk, rows_at(frame, 256)].T

    def activate(pre, center, slot, recon_slot, chunk):
        gate = 0.5 * jnp.tanh(0.5 * pre) + 0.5
        silu = pre * gate
        value = (turned[positions(center, chunk)].astype(F32) + silu).astype(jnp.bfloat16)
        hidden[positions(slot, chunk)] = value
        slopes[positions(slot, chunk)] = gate + silu * (1.0 - gate)
        recon[chunk, rows_at(recon_slot, 48)] = dot_nt(ow[...], value).astype(jnp.bfloat16)

    def decode(local, chunk):
        window = jnp.concatenate([turned[positions(local + tap, chunk)] for tap in range(3)], axis=1)
        weight = [
            conv_t[256 * block : 256 * block + 256]
            * jnp.full((1, 256), tap_mask(local, 2 - block), F32).astype(jnp.bfloat16)
            for block in range(3)
        ]
        pre = dot(window, jnp.concatenate(weight, axis=0))
        activate(pre, local + 2, local, local + 4, chunk)

    def decode_inner(chunk):
        mine, other = 1 + 4 * core, 5 - 4 * core
        own_copy(chunk).wait()
        for offset in range(4):
            turn(mine + offset, chunk)
        decode(mine, chunk)
        decode(mine + 1, chunk)
        core_copy(chunk).wait_recv()
        for offset in range(4):
            turn(other + offset, chunk)
        for local in (3, 4, other, other + 1):
            decode(local, chunk)

        @pl.when(clip_start)
        def _():
            activate(dot(turned[positions(1, chunk)], conv_t[512:768]), 1, 8, 3, chunk)

    def decode_halo(chunk):
        await_halo(chunk)
        for frame in (0, 9):
            turn(frame, chunk)
        for local in (0, 7):
            decode(local, chunk)
        send_recon(chunk)

    def first_layer(local, chunk):
        pre = dot(recon[chunk, rows_at(local + 3, 48, 3)].T, fwt[...])
        if 0 <= local < 7:
            value = jnp.maximum(pre, 0.2 * pre)
        else:
            on = valid(local)
            value = pre * jnp.where(pre > 0, on, 0.2 * on)
        value = value.astype(jnp.bfloat16)
        disc[rows_at(local + 3, SC)] = value
        if -1 <= local < 9:
            disc_t[rows_at(local + 1, 256)] = value.T

    def second_layer(local):
        window = jnp.concatenate([disc[rows_at(local + 2 + tap, SC)] for tap in range(3)], axis=1)
        pre = dot(window, second_t[...])
        act = jnp.maximum(pre, 0.2 * pre)
        logits = jnp.sum(act * head, axis=1, keepdims=True)
        scale = -sign * loss_scale * (1.0 if 0 <= local < 7 else valid(local))
        signed = sign * logits
        small = jnp.exp(-jnp.abs(signed))
        one_over = pl.reciprocal(1.0 + small, approx=True)
        one_over = one_over * (2.0 - (1.0 + small) * one_over)
        grad = scale * jnp.where(signed > 0, small * one_over, one_over)
        if -1 <= local < 8:
            share = grad * jnp.where(clip_start, 1.0, 0.0).astype(F32) if local < 0 else grad
            acc_head[...] += jnp.sum((act * share).reshape(SC // 8, 8, 256), axis=0)
        second[rows_at(local + 2, SC)] = (jnp.where(pre > 0, head, 0.2 * head) * grad).astype(jnp.bfloat16)

    def first_back(local):
        window = jnp.concatenate([second[rows_at(local + 3 - tap, SC)] for tap in range(3)], axis=1)
        back = dot(window, second_w[...].reshape(768, 256))
        on = 1.0 if 0 <= local < 7 else valid(local)
        slope = jnp.where(disc[rows_at(local + 3, SC)].astype(F32) > 0, on, 0.2 * on)
        value = (back * slope).astype(jnp.bfloat16)
        first[rows_at(local + 1, SC)] = value
        parts[rows_at((local + 1) % 5, 144)] = dot_nt(fwt[...], value)

    def recon_back(local, where):
        total = (
            parts[pl.ds((local + 2) % 5 * 144, 48)]
            + parts[pl.ds((local + 1) % 5 * 144 + 48, 48)]
            + parts[pl.ds(local % 5 * 144 + 96, 48)]
        )
        rgrad[rows_at(local, 48), where] = total.astype(jnp.bfloat16)

    def recon_back_first(where):
        rgrad[rows_at(8, 48), where] = (parts[144:192] + parts[48:96]).astype(jnp.bfloat16)

    def wide(blocks):
        return jnp.concatenate(blocks, axis=1)

    def weight_grads(chunk):
        own, where = range(8), cols(chunk)
        left = wide([disc_t[t * 256 : t * 256 + 768] for t in own])
        acc_second[...] += dot(left, second[2 * SC : 10 * SC])
        left = wide([recon[chunk, (t + 3) * 48 : (t + 6) * 48] for t in own])
        acc_first[...] += dot(left, first[SC : 9 * SC])
        value = jnp.concatenate([hidden[positions(t, chunk)] for t in own], axis=0)
        acc_out[...] += dot(wide([rgrad[t * 48 : t * 48 + 48, where] for t in own]), value)

        @pl.when(clip_start)
        def _():
            acc_second[256:768] += dot(disc_t[0:512], second[SC : 2 * SC])
            acc_first[48:144] += dot(recon[chunk, 144:240], first[0:SC])
            acc_out[...] += dot(rgrad[384:432, where], hidden[positions(8, chunk)])

    decode_inner(0)
    decode_halo(0)
    for chunk in range(1, NCH):
        decode_inner(chunk)

    for chunk in range(NCH):
        where = cols(chunk)
        await_recon(chunk)
        if chunk + 1 < NCH:
            send_halo(chunk + 1)
        for step in range(-3, 14):
            if step < 11:
                first_layer(step, chunk)
            if -2 <= step - 2 < 10:
                second_layer(step - 2)
            if -1 <= step - 4 < 9:
                first_back(step - 4)
            if step == 5:
                recon_back_first(where)
            if 0 <= step - 6:
                recon_back(step - 6, where)
        if chunk + 1 < NCH:
            decode_halo(chunk + 1)
        weight_grads(chunk)

    for part in range(3):
        grads1[part, 0:256] = acc_second[256 * part : 256 * part + 256].T
        grads1[part, 256:304] = acc_first[48 * part : 48 * part + 48]
        grads1[part, 304:320] = acc_out[16 * part : 16 * part + 16]
        grads1[part, 320:384] = jnp.zeros((64, 256), F32)
    grads1[0, 320:328] = jnp.broadcast_to(jnp.sum(acc_head[...], axis=0, keepdims=True), (8, 256))

    reduce1 = Reducer(place, grads1, total, 0, bufs[:3], send1, recv1)
    reduce2 = Reducer(place, grads2, total, 384, bufs[3:], send2, recv2)
    steps1, steps2 = reduce1.steps(), reduce2.steps()

    acc_conv = acc_second

    def conv_back(local):
        back = dot(rgrad[rows_at(local, 48)].T, ow[...])
        delta = (back * slopes[rows_at(local, WIDTH)]).astype(jnp.bfloat16)
        result = dot(wide([frames[chunk, rows_at(local, 256, 3)] for chunk in range(NCH)]), delta)
        for block, tap in ((0, 2), (1, 1), (2, 0)):
            rows = slice(256 * block, 256 * block + 256)
            acc_conv[rows] += result[rows] * tap_mask(local, tap)

    def conv_back_first():
        back = dot(rgrad[rows_at(8, 48)].T, ow[...])
        delta = (back * slopes[rows_at(8, WIDTH)]).astype(jnp.bfloat16)
        acc_conv[512:768] += dot(wide([frames[chunk, 256:512] for chunk in range(NCH)]), delta)

    steps1[0]()
    acc_conv[...] = jnp.zeros_like(acc_conv)

    def conv_back_pair(pair, carry):
        conv_back(2 * pair)
        conv_back(2 * pair + 1)
        return carry

    lax.fori_loop(0, 3, conv_back_pair, 0)
    steps1[1]()
    conv_back_pair(3, 0)
    pl.when(clip_start)(conv_back_first)
    for tap in range(3):
        grads2[tap] = acc_conv[256 * (2 - tap) : 256 * (2 - tap) + 256].T
        reduce2.scatter_send(tap)
    steps1[2]()
    steps2[1]()
    steps1[3]()
    steps2[2]()
    steps1[4]()
    steps2[3]()
    steps2[4]()

    reduce1.finish()
    reduce2.finish()
    for chunk in range(NCH):
        core_copy(chunk).wait_send()

        each_halo(chunk, lambda copy: copy.wait_send())
        to_both_sides(low_copy(chunk), high_copy(chunk), lambda copy: copy.wait_send())


def per_device(
    features, conv_weight, out_weight, first_weight, second_weight, head_weight, span_lengths, labels
):
    clips, frame_count, channels, positions = features.shape
    total_count = (
        clips * lax.axis_size("dp") * lax.axis_size("group") * frame_count * lax.axis_size("tm") * positions
    )
    loss_scale = float(total_count) ** (-0.5)
    bf16 = jnp.bfloat16
    operands = (
        span_lengths,
        labels,
        features.reshape(frame_count * channels, positions),
        conv_weight,
        out_weight,
        jnp.swapaxes(first_weight, 1, 2).reshape(144, 256),
        second_weight,
        head_weight.reshape(1, 256),
    )
    smem, vmem = pl.BlockSpec(memory_space=pltpu.SMEM), pl.BlockSpec(memory_space=pltpu.VMEM)
    dma = pltpu.SemaphoreType.DMA
    total = pl.pallas_call(
        functools.partial(block_kernel, loss_scale),
        out_shape=jax.ShapeDtypeStruct((3, 640, 256), bf16),
        in_specs=[smem, smem, pl.BlockSpec(memory_space=pl.ANY)] + [vmem] * 5,
        out_specs=vmem,
        scratch_shapes=[
            pltpu.VMEM((NCH, 2560, SC), bf16),
            pltpu.VMEM((10 * WIDTH, 256), bf16),
            pltpu.VMEM((9 * WIDTH, 256), bf16),
            pltpu.VMEM((9 * WIDTH, 256), F32),
            pltpu.VMEM((NCH, 768, SC), bf16),
            pltpu.VMEM((14 * SC, 256), bf16),
            pltpu.VMEM((10 * 256, SC), bf16),
            pltpu.VMEM((12 * SC, 256), bf16),
            pltpu.VMEM((10 * SC, 256), bf16),
            pltpu.VMEM((5 * 144, SC), F32),
            pltpu.VMEM((9 * 48, WIDTH), bf16),
            pltpu.VMEM((768, 256), bf16),
            pltpu.VMEM((768, 256), bf16),
            pltpu.VMEM((768, 256), F32),
            pltpu.VMEM((144, 256), F32),
            pltpu.VMEM((48, 256), F32),
            pltpu.VMEM((8, 256), F32),
            pltpu.VMEM((3, 384, 256), F32),
            pltpu.VMEM((3, 256, 256), F32),
            dma((NCH,)),
            dma((NCH,)),
            dma((NCH,)),
            dma((NCH, 2)),
            dma((NCH,)),
            dma((NCH, 2)),
            dma((NCH,)),
            dma((NCH,)),
            dma((NCH,)),
            dma((NCH,)),
            dma((NCH,)),
            dma((N_SLOTS,)),
            dma((N_SLOTS,)),
            dma((N_SLOTS,)),
            dma((N_SLOTS,)),
        ]
        + reduce_scratch(384)
        + reduce_scratch(256),
        compiler_params=pltpu.CompilerParams(
            collective_id=0, has_side_effects=True, vmem_limit_bytes=55 * MIB
        ),
    )(*operands)
    conv, out, first, second, head = pl.pallas_call(
        finish_kernel,
        out_shape=(
            jax.ShapeDtypeStruct((3, 256, 256), F32),
            jax.ShapeDtypeStruct((48, 256), F32),
            jax.ShapeDtypeStruct((3, 48, 256), F32),
            jax.ShapeDtypeStruct((3, 256, 256), F32),
            jax.ShapeDtypeStruct((1, 256), F32),
        ),
        in_specs=[vmem],
        out_specs=(vmem,) * 5,
        compiler_params=pltpu.CompilerParams(vmem_limit_bytes=16 * MIB),
    )(total)
    return conv, out, jnp.swapaxes(first, 1, 2), second, head.reshape(256)


def solution(mesh):
    placed = (
        P(("dp", "group"), "tm", None, None),
        P(),
        P(),
        P(),
        P(),
        P(),
        P(("dp", "group"), None),
        P(("dp", "group")),
    )
    return jax.shard_map(
        per_device, mesh=mesh, in_specs=placed, out_specs=(P(), P(), P(), P(), P()), check_vma=False
    )
```
